256 devices in a mesh: gz: 4 (over x), row: 4 (over y), col: 16 (over z, core).
Axes of the slice: x: 4, y: 4, z: 8, core: 2. Of those that a mesh axis runs over, the one named last changes fastest.
Arguments:
- leaf_rhs: float32 [512, 256, 512], P(('gz', 'col')), may hold values from -6 to 6
- leaf_inv: bfloat16 [512, 512, 512], P(('gz', 'col'), 'row'), as said below
- leaf_lower_mid: bfloat16 [512, 512, 512], P(('gz', 'col'), None, 'row'), may hold values from -0.09375 to 0.09375
- leaf_lower_coupling: bfloat16 [512, 3, 512, 512], P(('gz', 'col'), None, None, 'row'), may hold values from -0.015625 to 0.015625
- leaf_parent: int32 [512], P(('gz', 'col')), may hold values from 0 to 15
- leaf_pattern: int32 [512, 3], P(('gz', 'col')), may hold values 0 or 1
- mid_rhs: float32 [64, 256, 512], P(('gz', 'col')), may hold values from -6 to 6
- parent_diagonal_inverse: bfloat16 [64, 512, 512], P(('gz', 'col'), 'row'), as said below
- mid_lower: bfloat16 [64, 3, 512, 512], P(('gz', 'col'), None, None, 'row'), may hold values from -0.046875 to 0.046875
- mid_pattern: int32 [64, 2], P(('gz', 'col')), may hold values 0 or 1
- top_rhs: float32 [4, 256, 512], P('gz'), may hold values from -6 to 6
- top_inv: bfloat16 [4, 512, 512], P('gz', 'row'), as said below
- top_lower: bfloat16 [4, 2, 512, 512], P('gz', None, None, 'row'), may hold values from -0.1875 to 0.1875
- apex_rhs: float32 [3, 256, 512], replicated, may hold values from -6 to 6
- apex_inv: bfloat16 [3, 512, 512], P(None, 'row'), as said below
- apex_lower: bfloat16 [2, 512, 512], P(None, None, 'row'), may hold values from -0.25 to 0.25
Outputs:
- leaf_solution: float32 [512, 256, 512], P(('gz', 'col'), None, 'row')
- mid_solution: float32 [64, 256, 512], P(('gz', 'col'), None, 'row')
- top_solution: float32 [4, 256, 512], P('gz', None, 'row')
- apex_solution: float32 [3, 256, 512], P(None, 'gz', 'row')
The draws below stay inside these ranges and needn't reach their ends.
Inputs may be any that keep to these rules, and one draw needn't show every extreme that they name: `leaf_inv`: each diagonal-block inverse is lower triangular with a unit diagonal. `parent_diagonal_inverse`: lower triangular with a unit diagonal. `top_inv`: lower triangular with a unit diagonal. `apex_inv`: lower triangular with a unit diagonal.
All inputs are finite; a program needn't handle non-finite values. No bound on the sum of `leaf_pattern` or of `mid_pattern` on one device may be relied on, other than what follows from the above.
Results may differ from the reference program's by a relative error of at most 0.015.
Values may be sent and summed in bfloat16 or wider, within the bound.
A program may use at most 128 MiB of HBM per device.

```python
import jax
import jax.numpy as jnp
from jax import lax

B = 512
R = 256
LEAF_DEV = 8
LEAVES = 512
MIDS = 64
N_GZ = 4
N_COL = 16


def unit_lower(values):
    row_ids = lax.broadcasted_iota(jnp.int32, (B, B), 0)
    col_ids = lax.broadcasted_iota(jnp.int32, (B, B), 1)
    below = jnp.where(row_ids > col_ids, values * (0.7 / B ** 0.5), 0.0)
    return (below + jnp.where(row_ids == col_ids, 1.0, 0.0)).astype(jnp.bfloat16)


def draw_leaf_inv(key, part):
    key = jax.random.fold_in(key, 11)
    values = jax.random.normal(key, (LEAVES, B, B), jnp.float32)
    return unit_lower(values)


def draw_parent_diagonal_inverse(key, part):
    key = jax.random.fold_in(key, 12)
    values = jax.random.normal(key, (MIDS, B, B), jnp.float32)
    return unit_lower(values)


def draw_top_inv(key, part):
    key = jax.random.fold_in(key, 13)
    values = jax.random.normal(key, (N_GZ, B, B), jnp.float32)
    return unit_lower(values)


def draw_apex_inv(key, part):
    key = jax.random.fold_in(key, 14)
    values = jax.random.normal(key, (3, B, B), jnp.float32)
    return unit_lower(values)


def touch_ends(result, stream_key, least, high):
    place = [jax.random.randint(jax.random.fold_in(stream_key, axis), (), 0, length) for axis, length in enumerate(result.shape)]
    main_axis = result.shape.index(max(result.shape))
    beside = place[:main_axis] + [(place[main_axis] + 1) % result.shape[main_axis]] + place[main_axis + 1:]
    return result.at[tuple(place)].set(least).at[tuple(beside)].set(high)


def shard_levels(rng, extent, pieces, least, top_value):
    gain = 1.0
    for dim, shards_of in pieces:
        heights = jax.random.uniform(jax.random.fold_in(jax.random.fold_in(rng, 6), dim), (shards_of,), jnp.float32, least / len(pieces), top_value / len(pieces))
        gain = gain * jnp.repeat(jnp.exp(heights), extent[dim] // shards_of).reshape((-1,) + (1,) * (len(extent) - 1 - dim))
    return gain


def gaussian(rng, extent, deviation, reach, cuts=(), kind=jnp.bfloat16):
    result = deviation * jax.random.normal(rng, extent, jnp.float32)
    if cuts:
        result = result * shard_levels(rng, extent, cuts, -0.22, 0.18)
    return jnp.clip(result, -reach, reach).astype(kind)


def setup_inputs(seed: int = 0) -> dict:
    key_list = jax.random.split(jax.random.key(seed), 17)
    leaf_rhs = gaussian(key_list[0], (LEAVES, R, B), 1.0, 6.0, ((0, 64),), jnp.float32)
    leaf_inv = draw_leaf_inv(jax.random.fold_in(key_list[16], 71), 0)
    leaf_lower_mid = gaussian(key_list[2], (LEAVES, B, B), (B * LEAF_DEV) ** -0.5, 0.09375, ((0, 64), (2, 4)))
    leaf_lower_coupling = gaussian(key_list[3], (LEAVES, 3, B, B), (B * LEAF_DEV * N_COL * 2) ** -0.5, 0.015625, ((0, 64), (3, 4)))
    leaf_parent = touch_ends(jax.random.randint(key_list[4], (LEAVES,), 0, N_COL), jax.random.fold_in(key_list[4], 1), 0, N_COL - 1).astype(jnp.int32)
    leaf_pattern = touch_ends((jax.random.randint(key_list[5], (LEAVES, 3), 0, 2) < 1).astype(jnp.int32), jax.random.fold_in(key_list[5], 1), 0, 1)
    mid_rhs = gaussian(key_list[6], (MIDS, R, B), 1.0, 6.0, ((0, 64),), jnp.float32)
    parent_diagonal_inverse = draw_parent_diagonal_inverse(jax.random.fold_in(key_list[16], 71), 0)
    mid_lower = gaussian(key_list[8], (MIDS, 3, B, B), (B * N_COL * 2) ** -0.5, 0.046875, ((0, 64), (3, 4)))
    mid_pattern = touch_ends((jax.random.randint(key_list[9], (MIDS, 2), 0, 2) < 1).astype(jnp.int32), jax.random.fold_in(key_list[9], 1), 0, 1)
    top_rhs = gaussian(key_list[10], (N_GZ, R, B), 1.0, 6.0, ((0, 4),), jnp.float32)
    top_inv = draw_top_inv(jax.random.fold_in(key_list[16], 71), 0)
    top_lower = gaussian(key_list[12], (N_GZ, 2, B, B), (B * 2) ** -0.5, 0.1875, ((0, 4), (3, 4)))
    apex_rhs = gaussian(key_list[13], (3, R, B), 1.0, 6.0, (), jnp.float32)
    apex_inv = draw_apex_inv(jax.random.fold_in(key_list[16], 71), 0)
    apex_lower = gaussian(key_list[15], (2, B, B), B ** -0.5, 0.25, ((2, 4),))
    return {"leaf_rhs": leaf_rhs, "leaf_inv": leaf_inv, "leaf_lower_mid": leaf_lower_mid, "leaf_lower_coupling": leaf_lower_coupling, "leaf_parent": leaf_parent, "leaf_pattern": leaf_pattern, "mid_rhs": mid_rhs, "parent_diagonal_inverse": parent_diagonal_inverse, "mid_lower": mid_lower, "mid_pattern": mid_pattern, "top_rhs": top_rhs, "top_inv": top_inv, "top_lower": top_lower, "apex_rhs": apex_rhs, "apex_inv": apex_inv, "apex_lower": apex_lower}


def solve_one(items):
    inverse, right = items
    return jnp.dot(right.astype(jnp.bfloat16), inverse.T, preferred_element_type=jnp.float32)


def three_terms(items):
    solved, blocks = items
    return jnp.stack([jnp.dot(solved, blocks[k].T, preferred_element_type=jnp.float32) for k in range(blocks.shape[0])])


def reference(leaf_rhs, leaf_inv, leaf_lower_mid, leaf_lower_coupling, leaf_parent, leaf_pattern, mid_rhs, parent_diagonal_inverse, mid_lower, mid_pattern, top_rhs, top_inv, top_lower, apex_rhs, apex_inv, apex_lower):
    leaf_solved = lax.map(solve_one, (leaf_inv, leaf_rhs))
    leaf_round = leaf_solved.astype(jnp.bfloat16)

    def leaf_terms(items):
        solved, lower_mid, lower_up = items
        toward_parent = jnp.dot(solved, lower_mid.T, preferred_element_type=jnp.float32)
        return toward_parent, three_terms((solved, lower_up))

    toward_parent, to_up = lax.map(leaf_terms, (leaf_round, leaf_lower_mid, leaf_lower_coupling))
    to_up = to_up * leaf_pattern.astype(jnp.float32)[:, :, None, None]
    layer_lookup = jnp.arange(LEAVES, dtype=jnp.int32) // (LEAF_DEV * N_COL)
    mid_index = (layer_lookup * N_COL + leaf_parent).astype(jnp.int32)
    mid_total = mid_rhs - jax.ops.segment_sum(toward_parent, mid_index, num_segments=MIDS)
    parent_unknowns = lax.map(solve_one, (parent_diagonal_inverse, mid_total))
    mid_round = parent_unknowns.astype(jnp.bfloat16)
    mid_up = lax.map(three_terms, (mid_round, mid_lower))
    mid_weight = jnp.concatenate([jnp.ones((MIDS, 1), jnp.float32), mid_pattern.astype(jnp.float32)], axis=1)
    mid_up = mid_up * mid_weight[:, :, None, None]
    mid_layer = jnp.arange(MIDS, dtype=jnp.int32) // N_COL
    top_total = top_rhs - jax.ops.segment_sum(to_up[:, 0], layer_lookup, num_segments=N_GZ) - jax.ops.segment_sum(mid_up[:, 0], mid_layer, num_segments=N_GZ)
    top_solved = lax.map(solve_one, (top_inv, top_total))
    top_round = top_solved.astype(jnp.bfloat16)
    top_up = lax.map(three_terms, (top_round, top_lower))
    top_pair = jnp.arange(N_GZ, dtype=jnp.int32) // 2
    front_total = apex_rhs[:2] - jax.ops.segment_sum(to_up[:, 1], layer_lookup // 2, num_segments=2)
    front_total = front_total - jax.ops.segment_sum(mid_up[:, 1], mid_layer // 2, num_segments=2)
    front_total = front_total - jax.ops.segment_sum(top_up[:, 0], top_pair, num_segments=2)
    front_solved = lax.map(solve_one, (apex_inv[:2], front_total))
    front_round = front_solved.astype(jnp.bfloat16)
    front_up = jnp.dot(front_round[0], apex_lower[0].T, preferred_element_type=jnp.float32) + jnp.dot(front_round[1], apex_lower[1].T, preferred_element_type=jnp.float32)
    last_total = apex_rhs[2] - jnp.sum(to_up[:, 2], axis=0) - jnp.sum(mid_up[:, 2], axis=0) - jnp.sum(top_up[:, 1], axis=0) - front_up
    last_solved = solve_one((apex_inv[2], last_total))
    apex_unknowns = jnp.concatenate([front_solved, last_solved[None]], axis=0)
    return leaf_solved, parent_unknowns, top_solved, apex_unknowns
```

```python
import jax
import jax.numpy as jnp
from jax import lax
from jax.experimental import pallas as pl
from jax.experimental.pallas import tpu as pltpu
from jax.sharding import PartitionSpec as P

MESH = pl.DeviceIdType.MESH
F32 = jnp.float32
BF16 = jnp.bfloat16
N_LEAF = 8
SLICE = 128
HALF = 128
SHARE = 16


def dot_nt(a, b):
    return lax.dot_general(a, b, (((1,), (1,)), ((), ())), preferred_element_type=F32)


def send(src, dst, send_sem, recv_sem, where):
    return pltpu.make_async_remote_copy(
        src_ref=src,
        dst_ref=dst,
        send_sem=send_sem,
        recv_sem=recv_sem,
        device_id=where,
        device_id_type=MESH,
    )


def kernel(
    parent_s,
    pattern_s,
    midpat_s,
    rhs_h,
    inv_h,
    lm_h,
    lc_h,
    midrhs_h,
    pinv_h,
    midl_h,
    toprhs_h,
    topinv_h,
    topl_h,
    apexrhs_h,
    apexinv_h,
    apexl_h,
    leaf_o,
    mid_o,
    top_o,
    apex_o,
    rhs_v,
    inv_v,
    lm_v,
    lc_v,
    midrhs_v,
    pinv_v,
    midl_v,
    toprhs_v,
    topinv_v,
    topl_v,
    apexrhs_v,
    apexinv_v,
    apexl_v,
    sol_v,
    rnd_v,
    masked_v,
    up_v,
    yopp_v,
    yfwd_v,
    ybwd_v,
    yown_v,
    y1_v,
    ysend_v,
    y2_v,
    part_v,
    sib_v,
    pid_v,
    pidsib_v,
    acc_v,
    zsend_v,
    zrecv_v,
    mt_v,
    msol_v,
    csend_v,
    crecv_v,
    ownp_v,
    zsc_v,
    zin_v,
    rsend_v,
    rrecv_v,
    tops_v,
    q1_v,
    q1r_v,
    e_v,
    er_v,
    u_v,
    ur_v,
    fsend_v,
    fother_v,
    fins_v,
    fin_v,
    ld_leaf,
    ld_misc,
    out_leaf,
    out_misc,
    y1_ss,
    y1_rs,
    y2_ss,
    y2_rs,
    sib_ss,
    sib_rs,
    pid_sem,
    z_ss,
    z_rs,
    mt_ss,
    mt_rs,
    c_ss,
    c_rs,
    zin_ss,
    zin_rs,
    x_ss,
    x_rs,
):
    g = lax.axis_index("gz")
    r = lax.axis_index("row")
    c = lax.axis_index("col")
    z, core = c // 2, c % 2
    pair = g // 2
    block = core * 128 + z * SHARE
    sibling = {"col": 2 * z + (1 - core)}

    def rows(start, count, unit):
        return pl.ds(pl.multiple_of(start, unit), count)

    barrier = pltpu.get_barrier_semaphore()

    def greet(where):
        pl.semaphore_signal(barrier, inc=1, device_id=where, device_id_type=MESH)

    for apart in range(1, 16):
        greet({"col": (c + apart) % 16})
    for apart in range(1, 16):
        greet({"gz": (g + apart // 4) % 4, "row": (r + apart % 4) % 4})
    for i in range(4):
        giver = 2 * ((g % 2) * 4 + i) + g // 2
        greet({"gz": (g + 1 + ((c - giver + 16) % 16) // 4) % 4, "col": giver})

    def leaf_loads(l):
        return (
            pltpu.make_async_copy(rhs_h.at[l], rhs_v.at[l], ld_leaf.at[l, 0]),
            pltpu.make_async_copy(inv_h.at[l], inv_v.at[l], ld_leaf.at[l, 1]),
            pltpu.make_async_copy(lm_h.at[l], lm_v.at[l], ld_leaf.at[l, 2]),
        )

    def coupling_load(l):
        return pltpu.make_async_copy(
            lc_h.at[l], lc_v.at[:, :, rows(l * SLICE, SLICE, SLICE)], ld_leaf.at[l, 3]
        )

    misc = (
        (midrhs_h.at[0, :, rows(r * SLICE, SLICE, SLICE)], midrhs_v),
        (pinv_h.at[0], pinv_v),
        (midl_h.at[0], midl_v),
        (toprhs_h.at[0, rows(block, SHARE, SHARE), :], toprhs_v),
        (topinv_h.at[0], topinv_v),
        (topl_h.at[0], topl_v),
        (apexrhs_h.at[pair, rows(block, SHARE, SHARE), :], apexrhs_v.at[0]),
        (apexrhs_h.at[2, rows(block, SHARE, SHARE), :], apexrhs_v.at[1]),
        (apexinv_h.at[pair], apexinv_v.at[0]),
        (apexinv_h.at[2], apexinv_v.at[1]),
        (apexl_h.at[pair], apexl_v),
    )
    misc = [pltpu.make_async_copy(s, d, ld_misc.at[i]) for i, (s, d) in enumerate(misc)]

    @pl.loop(0, N_LEAF)
    def _(l):
        for copy in leaf_loads(l):
            copy.start()

    @pl.loop(0, N_LEAF)
    def _(l):
        coupling_load(l).start()

    for copy in misc:
        copy.start()

    @pl.loop(0, N_LEAF)
    def _(l):
        pid_v[l] = jnp.full((8, 128), parent_s[l].astype(F32), F32)

    pl.semaphore_wait(barrier, 34)

    pid_copy = send(pid_v, pidsib_v, pid_sem.at[0], pid_sem.at[1], sibling)
    pid_copy.start()

    ahead, behind, across = (r + 1) % 4, (r + 3) % 4, (r + 2) % 4

    def y1_copies(l):
        return (
            send(
                yopp_v.at[l, pl.ds(0, HALF)], y1_v.at[l, 0], y1_ss.at[l, 0], y1_rs.at[l, 0],
                {"row": ahead},
            ),
            send(
                yopp_v.at[l, pl.ds(HALF, HALF)], y1_v.at[l, 1], y1_ss.at[l, 1], y1_rs.at[l, 1],
                {"row": behind},
            ),
        )

    def y2_copies(l):
        return (
            send(ysend_v.at[l, 0], y2_v.at[l, 0], y2_ss.at[l, 0], y2_rs.at[l, 0], {"row": ahead}),
            send(ysend_v.at[l, 1], y2_v.at[l, 1], y2_ss.at[l, 1], y2_rs.at[l, 1], {"row": behind}),
        )

    def sib_copy(l):
        return send(part_v.at[l], sib_v.at[l], sib_ss.at[l], sib_rs.at[l], sibling)

    def leaf_out(l):
        return pltpu.make_async_copy(sol_v.at[l], leaf_o.at[l], out_leaf.at[l])

    @pl.loop(0, N_LEAF)
    def _(l):
        load_rhs, load_inv, load_lm = leaf_loads(l)
        load_rhs.wait()
        load_inv.wait()
        solved = dot_nt(rhs_v[l].astype(BF16), inv_v[l])
        sol_v[l] = solved
        rounded = solved.astype(BF16)
        rnd_v[l] = rounded
        load_lm.wait()
        yopp_v[l] = dot_nt(rounded, lm_v[l, rows(across * SLICE, SLICE, SLICE), :]).astype(BF16)
        for copy in y1_copies(l):
            copy.start()
        leaf_out(l).start()
        yfwd_v[l] = dot_nt(rounded, lm_v[l, rows(ahead * SLICE, SLICE, SLICE), :])
        ybwd_v[l] = dot_nt(rounded, lm_v[l, rows(behind * SLICE, SLICE, SLICE), :])
        yown_v[l] = dot_nt(rounded, lm_v[l, rows(r * SLICE, SLICE, SLICE), :])

    @pl.loop(0, N_LEAF)
    def _(l):
        forward, backward = y1_copies(l)
        to_ahead, to_behind = y2_copies(l)
        forward.wait_recv()
        ysend_v[l, 0, :HALF] = (yfwd_v[l, :HALF] + y1_v[l, 0].astype(F32)).astype(BF16)
        ysend_v[l, 0, HALF:] = yfwd_v[l, HALF:].astype(BF16)
        to_ahead.start()
        backward.wait_recv()
        ysend_v[l, 1, :HALF] = ybwd_v[l, :HALF].astype(BF16)
        ysend_v[l, 1, HALF:] = (ybwd_v[l, HALF:] + y1_v[l, 1].astype(F32)).astype(BF16)
        to_behind.start()

    @pl.loop(0, N_LEAF)
    def _(l):
        coupling_load(l).wait()
        rounded = rnd_v[l].astype(F32)
        for k in range(3):
            weight = pattern_s[l, k].astype(F32)
            masked_v[k, :, rows(l * SLICE, SLICE, SLICE)] = (rounded * weight).astype(BF16)

    for k in range(3):
        up_v[k] = dot_nt(masked_v[k], lc_v[k])

    acc_v[...] = jnp.zeros_like(acc_v)

    def gather_parents(pids, terms):
        for t in range(8):
            wanted = (2 * t + core).astype(F32)
            hit = jnp.maximum(1.0 - jnp.abs(pids - wanted), 0.0)
            acc_v[t] += (terms.reshape(32, 8, 128) * hit[None]).reshape(256, 128)

    pid_copy.wait_recv()

    @pl.loop(0, N_LEAF)
    def _(l):
        for copy in y2_copies(l):
            copy.wait_recv()
        total = yown_v[l] + y2_v[l, 0].astype(F32) + y2_v[l, 1].astype(F32)
        part_v[l] = total.astype(BF16)
        sib_copy(l).start()
        gather_parents(pid_v[l], total)

        @pl.when(l > 0)
        def _():
            sib_copy(l - 1).wait_recv()
            gather_parents(pidsib_v[l - 1], sib_v[l - 1].astype(F32))

    sib_copy(N_LEAF - 1).wait_recv()
    gather_parents(pidsib_v[N_LEAF - 1], sib_v[N_LEAF - 1].astype(F32))

    def z_copy(way, dist, h):
        step = 1 if way == 0 else 7
        return send(
            zsend_v.at[way, dist - 1, h],
            zrecv_v.at[way, dist - 1, h],
            z_ss.at[way, dist - 1, h],
            z_rs.at[way, dist - 1, h],
            {"col": 2 * ((z + step) % 8) + core},
        )

    z_flows = []
    for dist in (4, 3, 2, 1):
        for late in (0, 1):
            for way in (0, 1):
                h = way if late else 1 - way
                if dist == 4 and not late:
                    continue
                z_flows.append((way, dist, h))
    for way, dist, h in z_flows:
        target = (z + dist) % 8 if way == 0 else (z + 8 - dist) % 8
        term = acc_v[target, h * HALF : (h + 1) * HALF]
        if (way, dist + 1, h) in z_flows:
            z_copy(way, dist + 1, h).wait_recv()
            term = term + zrecv_v[way, dist, h].astype(F32)
        zsend_v[way, dist - 1, h] = term.astype(BF16)
        z_copy(way, dist, h).start()

    def mt_copy(h, apart):
        return send(
            mt_v.at[r, h], mt_v.at[r, h], mt_ss.at[h, apart - 1], mt_rs.at[h, apart - 1],
            {"row": (r + apart) % 4},
        )

    def mt_arrival(h, apart):
        source = (r + 4 - apart) % 4
        return send(
            mt_v.at[source, h], mt_v.at[source, h], mt_ss.at[h, apart - 1],
            mt_rs.at[h, apart - 1], {"row": source},
        )

    misc[0].wait()
    for h in (0, 1):
        z_copy(0, 1, h).wait_recv()
        z_copy(1, 1, h).wait_recv()
        total = (
            midrhs_v[h * HALF : (h + 1) * HALF]
            - acc_v[z, h * HALF : (h + 1) * HALF]
            - zrecv_v[0, 0, h].astype(F32)
            - zrecv_v[1, 0, h].astype(F32)
        )
        mt_v[r, h] = total.astype(BF16)
        for apart in (1, 3, 2):
            mt_copy(h, apart).start()

    misc[1].wait()
    misc[2].wait()
    for h in (0, 1):
        for apart in (1, 2, 3):
            mt_arrival(h, apart).wait_recv()

    mid_weight = (None, midpat_s[0, 0].astype(F32), midpat_s[0, 1].astype(F32))

    def c_copy(k):
        return send(csend_v.at[k], crecv_v.at[k], c_ss.at[k], c_rs.at[k], sibling)

    def layer_half(h, store):
        right = jnp.concatenate([mt_v[i, h] for i in range(4)], axis=1)
        solved = dot_nt(right, pinv_v[...])
        msol_v[rows(h * HALF, HALF, HALF)] = solved
        rounded = solved.astype(BF16)
        for k in range(3):
            term = dot_nt(rounded, midl_v[k])
            if k:
                term = term * mid_weight[k]
            store(k, up_v[k, rows(h * HALF, HALF, HALF)] + term)

    def store_send(k, value):
        csend_v[k] = value.astype(BF16)
        c_copy(k).start()

    def store_own(k, value):
        ownp_v[k] = value

    layer_half(1 - core, store_send)
    layer_half(core, store_own)
    mid_out = pltpu.make_async_copy(msol_v, mid_o.at[0], out_misc.at[0])
    mid_out.start()

    def zin_copy(k, apart):
        target = (z + apart) % 8
        return send(
            zsc_v.at[k, rows(target * SHARE, SHARE, SHARE)], zin_v.at[k, apart - 1],
            zin_ss.at[k], zin_rs.at[k], {"col": 2 * target + core},
        )

    def all_of(buffer, send_sem, recv_sem):
        return send(buffer, buffer, send_sem, recv_sem, {"row": ahead})

    for k in range(3):
        c_copy(k).wait_recv()
        total = ownp_v[k] + crecv_v[k].astype(F32)
        ownp_v[k] = total
        zsc_v[k] = total.astype(BF16)
        for apart in (4, 3, 5, 2, 6, 1, 7):
            zin_copy(k, apart).start()

    def share_sum(k):
        all_of(zin_v.at[k], zin_ss.at[k], zin_rs.at[k]).wait_recv()
        total = ownp_v[k, rows(z * SHARE, SHARE, SHARE)]
        for i in range(7):
            total = total + zin_v[k, i].astype(F32)
        return total

    own = share_sum(0)
    rsend_v[...] = own.astype(BF16)
    for apart in (2, 1, 3):
        send(rsend_v, rrecv_v.at[apart - 1], x_ss.at[0], x_rs.at[0], {"row": (r + apart) % 4}).start()
    for i in range(3, 11):
        misc[i].wait()
    p1 = share_sum(1)
    p2 = share_sum(2)
    all_of(rrecv_v, x_ss.at[0], x_rs.at[0]).wait_recv()
    for i in range(3):
        own = own + rrecv_v[i].astype(F32)
    solved = dot_nt((toprhs_v[...] - own).astype(BF16), topinv_v[...])
    rounded = solved.astype(BF16)
    tops_v[rows(block, SHARE, SHARE)] = solved
    q1 = p1 + dot_nt(rounded, topl_v[0])
    q1_v[...] = q1.astype(BF16)
    mate = g + 1 - 2 * (g % 2)
    facing = 3 - g

    def to_group(src, dst, sem, other):
        for layer in (1, 0):
            for apart in (2, 1, 3, 0):
                if layer or apart:
                    send(
                        src, dst.at[4 * layer + apart - 1], x_ss.at[sem], x_rs.at[sem],
                        {"gz": other if layer else g, "row": (r + apart) % 4},
                    ).start()

    to_group(q1_v, q1r_v, 1, mate)
    e = p2 + dot_nt(rounded, topl_v[1])
    e_v[...] = e.astype(BF16)
    for apart in range(15, 0, -1):
        send(
            e_v, er_v.at[apart - 1], x_ss.at[2], x_rs.at[2],
            {"gz": (g + apart // 4) % 4, "row": (r + apart % 4) % 4},
        ).start()
    for apart in range(1, 16):
        mine = tops_v.at[rows(block, SHARE, SHARE)]
        send(mine, mine, x_ss.at[3], x_rs.at[3], {"col": (c + apart) % 16}).start()

    all_of(q1r_v, x_ss.at[1], x_rs.at[1]).wait_recv()
    for i in range(7):
        q1 = q1 + q1r_v[i].astype(F32)
    front = dot_nt((apexrhs_v[0] - q1).astype(BF16), apexinv_v[0])
    fsend_v[...] = front
    u = dot_nt(front.astype(BF16), apexl_v[...])
    u_v[...] = u.astype(BF16)
    to_group(u_v, ur_v, 4, facing)
    send(fsend_v, fother_v, x_ss.at[5], x_rs.at[5], {"gz": facing}).start()
    fins_v[pair] = front

    all_of(er_v, x_ss.at[2], x_rs.at[2]).wait_recv()
    for i in range(15):
        e = e + er_v[i].astype(F32)
    all_of(tops_v.at[pl.ds(0, 240)], x_ss.at[3], x_rs.at[3]).wait_recv()
    top_out = pltpu.make_async_copy(tops_v, top_o.at[0], out_misc.at[1])
    top_out.start()
    last = apexrhs_v[1] - e - u

    all_of(fother_v, x_ss.at[5], x_rs.at[5]).wait_recv()
    fins_v[1 - pair] = fother_v[...]
    all_of(ur_v, x_ss.at[4], x_rs.at[4]).wait_recv()
    for i in range(7):
        last = last - ur_v[i].astype(F32)
    fins_v[2] = dot_nt(last.astype(BF16), apexinv_v[1])

    holder = core * 2 + z // 4
    turn = (g - holder + 7) % 4
    for i in range(4):
        send(
            fins_v, fin_v.at[:, rows((z % 4) * SHARE, SHARE, SHARE)], x_ss.at[6], x_rs.at[6],
            {"gz": holder, "col": (c + 4 * turn + i) % 16},
        ).start()

    pid_copy.wait_send()

    @pl.loop(0, N_LEAF)
    def _(l):
        for copy in y1_copies(l) + y2_copies(l) + (sib_copy(l),):
            copy.wait_send()
        leaf_out(l).wait()

    for way, dist, h in z_flows:
        z_copy(way, dist, h).wait_send()
    for h in (0, 1):
        for apart in (1, 2, 3):
            mt_copy(h, apart).wait_send()
    for k in range(3):
        c_copy(k).wait_send()
        all_of(zin_v.at[k], zin_ss.at[k], zin_rs.at[k]).wait_send()
    all_of(rrecv_v, x_ss.at[0], x_rs.at[0]).wait_send()
    all_of(q1r_v, x_ss.at[1], x_rs.at[1]).wait_send()
    all_of(er_v, x_ss.at[2], x_rs.at[2]).wait_send()
    all_of(tops_v.at[pl.ds(0, 240)], x_ss.at[3], x_rs.at[3]).wait_send()
    all_of(ur_v, x_ss.at[4], x_rs.at[4]).wait_send()
    all_of(fother_v, x_ss.at[5], x_rs.at[5]).wait_send()
    all_of(fin_v, x_ss.at[6], x_rs.at[6]).wait()
    apex_out = pltpu.make_async_copy(fin_v, apex_o, out_misc.at[2])
    apex_out.start()
    mid_out.wait()
    top_out.wait()
    apex_out.wait()


def per_device(*args):
    (
        leaf_rhs, leaf_inv, leaf_lower_mid, leaf_lower_coupling, leaf_parent, leaf_pattern,
        mid_rhs, parent_diagonal_inverse, mid_lower, mid_pattern, top_rhs, top_inv, top_lower,
        apex_rhs, apex_inv, apex_lower,
    ) = args
    smem = pl.BlockSpec(memory_space=pltpu.SMEM)
    anywhere = pl.BlockSpec(memory_space=pl.ANY)
    V = pltpu.VMEM
    D = pltpu.SemaphoreType.DMA
    scratch = [
        V((8, 256, 512), F32),
        V((8, 128, 512), BF16),
        V((8, 512, 128), BF16),
        V((3, 512, 1024), BF16),
        V((256, 128), F32),
        V((128, 512), BF16),
        V((3, 512, 128), BF16),
        V((16, 512), F32),
        V((128, 512), BF16),
        V((2, 512, 128), BF16),
        V((2, 16, 512), F32),
        V((2, 128, 512), BF16),
        V((512, 128), BF16),
        V((8, 256, 128), F32),
        V((8, 256, 128), BF16),
        V((3, 256, 1024), BF16),
        V((3, 256, 512), F32),
        V((8, 256, 128), BF16),
        V((8, 256, 128), F32),
        V((8, 256, 128), F32),
        V((8, 256, 128), F32),
        V((8, 2, 128, 128), BF16),
        V((8, 2, 256, 128), BF16),
        V((8, 2, 256, 128), BF16),
        V((8, 256, 128), BF16),
        V((8, 256, 128), BF16),
        V((8, 8, 128), F32),
        V((8, 8, 128), F32),
        V((8, 256, 128), F32),
        V((2, 4, 2, 128, 128), BF16),
        V((2, 4, 2, 128, 128), BF16),
        V((4, 2, 128, 128), BF16),
        V((256, 128), F32),
        V((3, 128, 512), BF16),
        V((3, 128, 512), BF16),
        V((3, 128, 512), F32),
        V((3, 128, 512), BF16),
        V((3, 7, 16, 512), BF16),
        V((16, 512), BF16),
        V((3, 16, 512), BF16),
        V((256, 128), F32),
        V((16, 512), BF16),
        V((7, 16, 512), BF16),
        V((16, 512), BF16),
        V((15, 16, 512), BF16),
        V((16, 512), BF16),
        V((7, 16, 512), BF16),
        V((16, 128), F32),
        V((16, 128), F32),
        V((3, 16, 128), F32),
        V((3, 64, 128), F32),
        D((8, 4)),
        D((11,)),
        D((8,)),
        D((3,)),
        D((8, 2)),
        D((8, 2)),
        D((8, 2)),
        D((8, 2)),
        D((8,)),
        D((8,)),
        D((2,)),
        D((2, 4, 2)),
        D((2, 4, 2)),
        D((2, 3)),
        D((2, 3)),
        D((3,)),
        D((3,)),
        D((3,)),
        D((3,)),
        D((7,)),
        D((7,)),
    ]
    return pl.pallas_call(
        kernel,
        out_shape=(
            jax.ShapeDtypeStruct((8, 256, 128), F32),
            jax.ShapeDtypeStruct((1, 256, 128), F32),
            jax.ShapeDtypeStruct((1, 256, 128), F32),
            jax.ShapeDtypeStruct((3, 64, 128), F32),
        ),
        in_specs=[smem] * 3 + [anywhere] * 13,
        out_specs=(anywhere,) * 4,
        scratch_shapes=scratch,
        compiler_params=pltpu.CompilerParams(
            collective_id=0, has_side_effects=True, vmem_limit_bytes=48 * 1024 * 1024
        ),
        name="tree_solve",
    )(
        leaf_parent, leaf_pattern, mid_pattern, leaf_rhs, leaf_inv, leaf_lower_mid,
        leaf_lower_coupling, mid_rhs, parent_diagonal_inverse, mid_lower, top_rhs, top_inv,
        top_lower, apex_rhs, apex_inv, apex_lower,
    )


def solution(mesh):
    placed = (
        P(("gz", "col"), None, None),
        P(("gz", "col"), "row", None),
        P(("gz", "col"), None, "row"),
        P(("gz", "col"), None, None, "row"),
        P(("gz", "col")),
        P(("gz", "col"), None),
        P(("gz", "col"), None, None),
        P(("gz", "col"), "row", None),
        P(("gz", "col"), None, None, "row"),
        P(("gz", "col"), None),
        P("gz", None, None),
        P("gz", "row", None),
        P("gz", None, None, "row"),
        P(),
        P(None, "row", None),
        P(None, None, "row"),
    )
    return jax.shard_map(
        per_device,
        mesh=mesh,
        in_specs=placed,
        out_specs=(
            P(("gz", "col"), None, "row"),
            P(("gz", "col"), None, "row"),
            P("gz", None, "row"),
            P(None, "gz", "row"),
        ),
        check_vma=False,
    )
```

```python
import jax
import jax.numpy as jnp
from jax import lax
from jax.experimental import pallas as pl
from jax.experimental.pallas import tpu as pltpu
from jax.sharding import PartitionSpec as P

MESH = pl.DeviceIdType.MESH
F32 = jnp.float32
BF16 = jnp.bfloat16
N_LEAF = 8
SLICE = 128
HALF = 128
ROWS_Y = 128
ROWS_Z = 256 - ROWS_Y
SHARE = 16


def dot_nt(a, b):
    return lax.dot_general(a, b, (((1,), (1,)), ((), ())), preferred_element_type=F32)


def send(src, dst, send_sem, recv_sem, where):
    return pltpu.make_async_remote_copy(
        src_ref=src,
        dst_ref=dst,
        send_sem=send_sem,
        recv_sem=recv_sem,
        device_id=where,
        device_id_type=MESH,
    )


def kernel(
    parent_s,
    pattern_s,
    midpat_s,
    rhs_h,
    inv_h,
    lm_h,
    lc_h,
    midrhs_h,
    pinv_h,
    midl_h,
    toprhs_h,
    topinv_h,
    topl_h,
    apexrhs_h,
    apexinv_h,
    apexl_h,
    leaf_o,
    mid_o,
    top_o,
    apex_o,
    rhs_v,
    inv_v,
    lm_v,
    lc_v,
    midrhs_v,
    pinv_v,
    midl_v,
    toprhs_v,
    topinv_v,
    topl_v,
    apexrhs_v,
    apexinv_v,
    apexl_v,
    sol_v,
    rnd_v,
    weight_v,
    pidrow_v,
    up_v,
    yopp_v,
    y1_v,
    ysend_v,
    y2_v,
    part_v,
    sib_v,
    pid_v,
    pidsib_v,
    acc_v,
    yz_s,
    yz_r,
    pairs_s,
    pairs_r,
    wide_v,
    zsum_s,
    zsum_r,
    rs_s,
    rs_r,
    mt_v,
    msol_v,
    csend_v,
    crecv_v,
    ownp_v,
    zsc_v,
    zin_v,
    rsend_v,
    rrecv_v,
    tops_v,
    q1_v,
    q1r_v,
    e_v,
    er_v,
    u_v,
    ur_v,
    fsend_v,
    fother_v,
    fins_v,
    fin_v,
    ld_leaf,
    ld_misc,
    out_leaf,
    out_misc,
    y1_ss,
    y1_rs,
    y2_ss,
    y2_rs,
    sib_ss,
    sib_rs,
    pid_sem,
    pairs_ss,
    pairs_rs,
    yz_sem,
    zsum_ss,
    zsum_rs,
    rs_ss,
    rs_rs,
    mt_ss,
    mt_rs,
    c_ss,
    c_rs,
    zin_ss,
    zin_rs,
    x_ss,
    x_rs,
):
    g = lax.axis_index("gz")
    r = lax.axis_index("row")
    c = lax.axis_index("col")
    z, core = c // 2, c % 2
    pair = g // 2
    mate = g + 1 - 2 * (g % 2)
    facing = 3 - g
    block = core * 128 + z * SHARE
    sibling = {"col": 2 * z + (1 - core)}
    ahead, behind, across = (r + 1) % 4, (r + 3) % 4, (r + 2) % 4
    y_half, z_half = ROWS_Y // 2, ROWS_Z // 2

    def rows(start, count, unit):
        return pl.ds(pl.multiple_of(start, unit), count)

    def slab(index):
        return rows(index * SLICE, SLICE, SLICE)

    barrier = pltpu.get_barrier_semaphore()

    def greet(where):
        pl.semaphore_signal(barrier, inc=1, device_id=where, device_id_type=MESH)

    greet(sibling)
    for apart in range(1, 8):
        greet({"col": 2 * ((z + apart) % 8) + core})
    for apart in range(1, 4):
        greet({"row": (r + apart) % 4})
    for apart in range(4):
        greet({"gz": mate, "row": (r + apart) % 4})
        greet({"gz": facing, "row": (r + apart) % 4})
    greet({"gz": (g + 2) % 4})
    for i in range(4):
        giver = 2 * ((g % 2) * 4 + i) + g // 2
        greet({"gz": (g + 1 + ((c - giver + 16) % 16) // 4) % 4, "col": giver})

    def leaf_loads(l):
        return (
            pltpu.make_async_copy(rhs_h.at[l], rhs_v.at[l], ld_leaf.at[l, 0]),
            pltpu.make_async_copy(inv_h.at[l], inv_v.at[l], ld_leaf.at[l, 1]),
        )

    def lower_load(l):
        return pltpu.make_async_copy(lm_h.at[l], lm_v.at[:, slab(l)], ld_leaf.at[l, 2])

    def coupling_load(l):
        return pltpu.make_async_copy(lc_h.at[l], lc_v.at[:, :, slab(l)], ld_leaf.at[l, 3])

    misc = (
        (midrhs_h.at[0, :, slab(r)], midrhs_v),
        (pinv_h.at[0], pinv_v),
        (midl_h.at[0], midl_v),
        (toprhs_h.at[0, rows(block, SHARE, SHARE), :], toprhs_v),
        (topinv_h.at[0], topinv_v),
        (topl_h.at[0], topl_v),
        (apexrhs_h.at[pair, rows(block, SHARE, SHARE), :], apexrhs_v.at[0]),
        (apexrhs_h.at[2, rows(block, SHARE, SHARE), :], apexrhs_v.at[1]),
        (apexinv_h.at[pair], apexinv_v.at[0]),
        (apexinv_h.at[2], apexinv_v.at[1]),
        (apexl_h.at[pair], apexl_v),
    )
    misc = [pltpu.make_async_copy(s, d, ld_misc.at[i]) for i, (s, d) in enumerate(misc)]

    @pl.loop(0, N_LEAF)
    def _(l):
        for copy in leaf_loads(l):
            copy.start()

    @pl.loop(0, N_LEAF)
    def _(l):
        lower_load(l).start()

    @pl.loop(0, N_LEAF)
    def _(l):
        coupling_load(l).start()

    for copy in misc:
        copy.start()

    @pl.loop(0, N_LEAF)
    def _(l):
        parent = parent_s[l].astype(F32)
        pid_v[l] = jnp.full((8, 128), parent, F32)
        pidrow_v[:, slab(l)] = jnp.full((16, 128), parent, F32)
        for k in range(3):
            weight_v[k, :, slab(l)] = jnp.full((16, 128), pattern_s[k, l].astype(F32), F32).astype(
                BF16
            )

    def leaf_out(l):
        return pltpu.make_async_copy(sol_v.at[l], leaf_o.at[l], out_leaf.at[l])

    @pl.loop(0, N_LEAF)
    def _(l):
        for copy in leaf_loads(l):
            copy.wait()
        solved = dot_nt(rhs_v[l].astype(BF16), inv_v[l])
        sol_v[l] = solved
        rnd_v[:, slab(l)] = solved.astype(BF16)
        leaf_out(l).start()

    pl.semaphore_wait(barrier, 24)

    pid_copy = send(pid_v, pidsib_v, pid_sem.at[0], pid_sem.at[1], sibling)
    pid_copy.start()

    def y1_copies(l):
        return (
            send(
                yopp_v.at[l, pl.ds(0, y_half)], y1_v.at[l, 0], y1_ss.at[l, 0], y1_rs.at[l, 0],
                {"row": ahead},
            ),
            send(
                yopp_v.at[l, pl.ds(y_half, y_half)], y1_v.at[l, 1], y1_ss.at[l, 1],
                y1_rs.at[l, 1], {"row": behind},
            ),
        )

    def y2_copies(l):
        return (
            send(ysend_v.at[l, 0], y2_v.at[l, 0], y2_ss.at[l, 0], y2_rs.at[l, 0], {"row": ahead}),
            send(ysend_v.at[l, 1], y2_v.at[l, 1], y2_ss.at[l, 1], y2_rs.at[l, 1], {"row": behind}),
        )

    def sib_copy(l):
        return send(part_v.at[l], sib_v.at[l], sib_ss.at[l], sib_rs.at[l], sibling)

    def to_mid(l, target):
        return dot_nt(rnd_v[:ROWS_Y, slab(l)], lm_v[slab(target), slab(l)])

    @pl.loop(0, N_LEAF)
    def _(l):
        lower_load(l).wait()
        yopp_v[l] = to_mid(l, across).astype(BF16)
        for copy in y1_copies(l):
            copy.start()

    def pairs_copy(t):
        return send(pairs_s.at[t], pairs_r.at[t], pairs_ss.at[t], pairs_rs.at[t], sibling)

    def masked(parent):
        hit = jnp.maximum(1.0 - jnp.abs(pidrow_v[...] - parent.astype(F32)), 0.0).astype(BF16)
        terms = rnd_v[ROWS_Y:].reshape(ROWS_Z // 16, 16, 1024) * hit[None]
        return terms.reshape(ROWS_Z, 1024)

    def in_turn(i):
        return (z + 4 + ((i + 1) // 2) * (1 - 2 * (i % 2))) % 8

    def pairs(first, last):
        @pl.loop(first, last)
        def _(i):
            t = in_turn(i)
            terms = jnp.concatenate([masked(2 * t + 1 - core), masked(2 * t + core)], axis=0)
            sums = dot_nt(terms, lm_v[...])
            pairs_s[t] = sums[:ROWS_Z].astype(BF16)
            pairs_copy(t).start()
            wide_v[t] = sums[ROWS_Z:]

    pairs(0, 3)

    def z_copy(buffers, way, dist, h):
        out, into, send_sem, recv_sem = buffers
        at = (way, dist - 1, h)
        step = 1 if way == 0 else 7
        return send(
            out.at[at], into.at[at], send_sem.at[at], recv_sem.at[at],
            {"col": 2 * ((z + step) % 8) + core},
        )

    zsum = (zsum_s, zsum_r, zsum_ss, zsum_rs)
    flows = [
        (way, dist, way if late else 1 - way)
        for dist in (4, 3, 2, 1)
        for late in (0, 1)
        for way in (0, 1)
        if late or dist < 4
    ]

    def z_step(buffers, term_of, group):
        for way, dist, h in group:
            target = (z + dist) % 8 if way == 0 else (z + 8 - dist) % 8
            term = term_of(target, h)
            if (way, dist + 1, h) in flows:
                z_copy(buffers, way, dist + 1, h).wait_recv()
                term = term + buffers[1][way, dist, h].astype(F32)
            buffers[0][way, dist - 1, h] = term.astype(BF16)
            z_copy(buffers, way, dist, h).start()

    def z_term(target, h):
        part = pl.ds(h * z_half, z_half)
        return wide_v[target, part] + pairs_r[target, part].astype(F32)

    def ready(t):
        pairs_copy(t % 8).wait_recv()

    ready(z + 4)
    z_step(zsum, z_term, flows[0:2])
    ready(z + 3)
    ready(z + 5)
    z_step(zsum, z_term, flows[2:4])

    @pl.loop(0, N_LEAF)
    def _(l):
        forward, backward = y1_copies(l)
        to_ahead, to_behind = y2_copies(l)
        term = to_mid(l, ahead)
        forward.wait_recv()
        ysend_v[l, 0, :y_half] = (term[:y_half] + y1_v[l, 0].astype(F32)).astype(BF16)
        ysend_v[l, 0, y_half:] = term[y_half:].astype(BF16)
        to_ahead.start()
        term = to_mid(l, behind)
        backward.wait_recv()
        ysend_v[l, 1, :y_half] = term[:y_half].astype(BF16)
        ysend_v[l, 1, y_half:] = (term[y_half:] + y1_v[l, 1].astype(F32)).astype(BF16)
        to_behind.start()

    pairs(3, 8)
    z_step(zsum, z_term, flows[4:6])

    @pl.loop(0, N_LEAF)
    def _(l):
        coupling_load(l).wait()

    for k in range(3):
        terms = rnd_v[...].reshape(16, 16, 1024) * weight_v[k][None]
        up_v[k] = dot_nt(terms.reshape(256, 1024), lc_v[k])

    ready(z + 2)
    ready(z + 6)
    z_step(zsum, z_term, flows[6:8])

    acc_v[...] = jnp.zeros_like(acc_v)

    def gather_parents(pids, terms):
        for t in range(8):
            wanted = (2 * t + core).astype(F32)
            hit = jnp.maximum(1.0 - jnp.abs(pids - wanted), 0.0)
            acc_v[t] += (terms.reshape(ROWS_Y // 8, 8, 128) * hit[None]).reshape(ROWS_Y, 128)

    def collect(first, last):
        @pl.loop(first, last)
        def _(l):
            term = to_mid(l, r)
            for copy in y2_copies(l):
                copy.wait_recv()
            total = term + y2_v[l, 0].astype(F32) + y2_v[l, 1].astype(F32)
            part_v[l] = total.astype(BF16)
            sib_copy(l).start()
            gather_parents(pid_v[l], total)

            @pl.when(l > 0)
            def _():
                sib_copy(l - 1).wait_recv()
                gather_parents(pidsib_v[l - 1], sib_v[l - 1].astype(F32))

    pid_copy.wait_recv()
    collect(0, 3)
    z_step(zsum, z_term, flows[8:10])
    collect(3, 6)
    ready(z + 1)
    ready(z + 7)
    z_step(zsum, z_term, flows[10:12])
    collect(6, N_LEAF)
    sib_copy(N_LEAF - 1).wait_recv()
    gather_parents(pidsib_v[N_LEAF - 1], sib_v[N_LEAF - 1].astype(F32))

    def yz_copy(apart):
        target = (z + apart) % 8
        return send(
            yz_s.at[target], yz_r.at[apart - 1], yz_sem.at[0], yz_sem.at[1],
            {"col": 2 * target + core},
        )

    yz_all = send(yz_r, yz_r, yz_sem.at[0], yz_sem.at[1], sibling)
    for apart in (4, 3, 5, 2, 6, 1, 7):
        target = (z + apart) % 8
        yz_s[target] = acc_v[target].astype(BF16)
        yz_copy(apart).start()
    z_step(zsum, z_term, flows[12:14])

    def rs_copy(apart):
        return send(
            rs_s.at[(r + apart) % 4], rs_r.at[apart - 1], rs_ss.at[apart - 1],
            rs_rs.at[apart - 1], {"row": (r + apart) % 4},
        )

    ready(z)
    for h in (0, 1):
        for way in (0, 1):
            z_copy(zsum, way, 1, h).wait_recv()
        total = z_term(z, h) + zsum_r[0, 0, h].astype(F32) + zsum_r[1, 0, h].astype(F32)
        wide_v[z, h * z_half : (h + 1) * z_half] = total
        for i in range(4):
            rs_s[i, h * z_half : (h + 1) * z_half] = total[:, i * SLICE : (i + 1) * SLICE].astype(
                BF16
            )
    for apart in (2, 1, 3):
        rs_copy(apart).start()

    parts = ((0, ROWS_Y), (ROWS_Y, ROWS_Z))

    def mt_copy(p, apart):
        mine = mt_v.at[r, pl.ds(*parts[p])]
        return send(
            mine, mine, mt_ss.at[p, apart - 1], mt_rs.at[p, apart - 1], {"row": (r + apart) % 4}
        )

    def mt_arrival(p, apart):
        source = (r + 4 - apart) % 4
        theirs = mt_v.at[source, pl.ds(*parts[p])]
        return send(
            theirs, theirs, mt_ss.at[p, apart - 1], mt_rs.at[p, apart - 1], {"row": source}
        )

    misc[0].wait()
    yz_all.wait_recv()
    total = midrhs_v[:ROWS_Y] - acc_v[z]
    for i in range(7):
        total = total - yz_r[i].astype(F32)
    mt_v[r, :ROWS_Y] = total.astype(BF16)
    for apart in (2, 1, 3):
        mt_copy(0, apart).start()
    for apart in (1, 2, 3):
        rs_copy(apart).wait_recv()
    total = midrhs_v[ROWS_Y:] - wide_v[z, :, slab(r)]
    for i in range(3):
        total = total - rs_r[i].astype(F32)
    mt_v[r, ROWS_Y:] = total.astype(BF16)
    for apart in (2, 1, 3):
        mt_copy(1, apart).start()

    mid_weight = (None, midpat_s[0, 0].astype(F32), midpat_s[0, 1].astype(F32))

    def c_copy(k):
        return send(csend_v.at[k], crecv_v.at[k], c_ss.at[k], c_rs.at[k], sibling)

    misc[1].wait()
    misc[2].wait()
    for h in (0, 1):
        for apart in (1, 2, 3):
            mt_arrival(h, apart).wait_recv()
        here = slice(h * HALF, (h + 1) * HALF)
        right = jnp.concatenate([mt_v[i, here] for i in range(4)], axis=1)
        solved = dot_nt(right, pinv_v[...])
        msol_v[here] = solved
        rounded = solved.astype(BF16)
        for k in range(3):
            term = dot_nt(rounded, midl_v[k])
            if k:
                term = term * mid_weight[k]
            up_v[k, here] = up_v[k, here] + term
            if h:
                csend_v[k] = up_v[k, rows((1 - core) * HALF, HALF, HALF)].astype(BF16)
                c_copy(k).start()
    mid_out = pltpu.make_async_copy(msol_v, mid_o.at[0], out_misc.at[0])
    mid_out.start()

    def zin_copy(k, apart):
        target = (z + apart) % 8
        return send(
            zsc_v.at[k, rows(target * SHARE, SHARE, SHARE)], zin_v.at[k, apart - 1],
            zin_ss.at[k], zin_rs.at[k], {"col": 2 * target + core},
        )

    def all_of(buffer, sem):
        return send(buffer, buffer, x_ss.at[sem], x_rs.at[sem], {"row": ahead})

    def zin_all(k):
        return send(zin_v.at[k], zin_v.at[k], zin_ss.at[k], zin_rs.at[k], {"row": ahead})

    for k in range(3):
        c_copy(k).wait_recv()
        total = up_v[k, rows(core * HALF, HALF, HALF)] + crecv_v[k].astype(F32)
        ownp_v[k] = total
        zsc_v[k] = total.astype(BF16)
        for apart in (4, 3, 5, 2, 6, 1, 7):
            zin_copy(k, apart).start()

    def share_sum(k):
        zin_all(k).wait_recv()
        total = ownp_v[k, rows(z * SHARE, SHARE, SHARE)]
        for i in range(7):
            total = total + zin_v[k, i].astype(F32)
        return total

    def to_rows(src, dst, sem):
        for apart in (2, 1, 3):
            send(
                src, dst.at[apart - 1], x_ss.at[sem], x_rs.at[sem], {"row": (r + apart) % 4}
            ).start()

    pid_copy.wait_send()

    @pl.loop(0, N_LEAF)
    def _(l):
        for copy in y1_copies(l) + y2_copies(l) + (sib_copy(l), pairs_copy(l)):
            copy.wait_send()
        leaf_out(l).wait()

    own = share_sum(0)
    rsend_v[...] = own.astype(BF16)
    to_rows(rsend_v, rrecv_v, 0)
    for i in range(3, 11):
        misc[i].wait()
    for way, dist, h in flows:
        z_copy(zsum, way, dist, h).wait_send()
    yz_all.wait_send()
    all_of(rrecv_v, 0).wait_recv()
    for i in range(3):
        own = own + rrecv_v[i].astype(F32)
    solved = dot_nt((toprhs_v[...] - own).astype(BF16), topinv_v[...])
    rounded = solved.astype(BF16)
    q1 = share_sum(1) + dot_nt(rounded, topl_v[0])
    q1_v[...] = q1.astype(BF16)

    def to_group(src, dst, sem, other):
        for layer in (1, 0):
            for apart in (2, 1, 3, 0):
                if layer or apart:
                    send(
                        src, dst.at[4 * layer + apart - 1], x_ss.at[sem], x_rs.at[sem],
                        {"gz": other if layer else g, "row": (r + apart) % 4},
                    ).start()

    to_group(q1_v, q1r_v, 1, mate)
    tops_v[rows(block, SHARE, SHARE)] = solved
    e = share_sum(2) + dot_nt(rounded, topl_v[1])
    e_v[0] = e.astype(BF16)
    to_rows(e_v.at[0], er_v.at[0], 2)
    for apart in range(1, 8):
        mine = tops_v.at[rows(block, SHARE, SHARE)]
        send(
            mine, mine, x_ss.at[3], x_rs.at[3], {"col": 2 * ((z + apart) % 8) + core}
        ).start()

    all_of(q1r_v, 1).wait_recv()
    for i in range(7):
        q1 = q1 + q1r_v[i].astype(F32)
    front = dot_nt((apexrhs_v[0] - q1).astype(BF16), apexinv_v[0])
    u = dot_nt(front.astype(BF16), apexl_v[...])
    u_v[...] = u.astype(BF16)
    to_group(u_v, ur_v, 4, facing)
    fsend_v[...] = front
    fins_v[pair] = front
    send(fsend_v, fother_v, x_ss.at[5], x_rs.at[5], {"gz": facing}).start()

    all_of(er_v.at[0], 2).wait_recv()
    for i in range(3):
        e = e + er_v[0, i].astype(F32)
    e_v[1] = e.astype(BF16)
    for apart in (1, 2, 3):
        send(
            e_v.at[1], er_v.at[1, apart - 1], x_ss.at[7], x_rs.at[7], {"gz": (g + apart) % 4}
        ).start()
    tops_seven = tops_v.at[rows(core * HALF, 112, HALF)]
    tops_eight = tops_v.at[rows(core * HALF, HALF, HALF)]
    tops_other = tops_v.at[rows((1 - core) * HALF, HALF, HALF)]
    all_of(tops_seven, 3).wait()
    tops_copy = send(tops_eight, tops_eight, x_ss.at[8], x_rs.at[8], sibling)
    tops_copy.start()
    for k in range(3):
        c_copy(k).wait_send()
        zin_all(k).wait_send()
    for p in (0, 1):
        for apart in (1, 2, 3):
            mt_copy(p, apart).wait_send()
    for apart in (1, 2, 3):
        rs_copy(apart).wait_send()
    all_of(rrecv_v, 0).wait_send()
    all_of(q1r_v, 1).wait_send()
    all_of(er_v.at[0], 2).wait_send()

    all_of(er_v.at[1], 7).wait_recv()
    for i in range(3):
        e = e + er_v[1, i].astype(F32)
    last = apexrhs_v[1] - e - u
    all_of(fother_v, 5).wait_recv()
    fins_v[1 - pair] = fother_v[...]
    all_of(ur_v, 4).wait_recv()
    for i in range(7):
        last = last - ur_v[i].astype(F32)
    fins_v[2] = dot_nt(last.astype(BF16), apexinv_v[1])

    holder = core * 2 + z // 4
    turn = (g - holder + 7) % 4
    for i in range(4):
        send(
            fins_v, fin_v.at[:, rows((z % 4) * SHARE, SHARE, SHARE)], x_ss.at[6], x_rs.at[6],
            {"gz": holder, "col": (c + 4 * turn + i) % 16},
        ).start()

    send(tops_eight, tops_other, x_ss.at[8], x_rs.at[8], sibling).wait_recv()
    top_out = pltpu.make_async_copy(tops_v, top_o.at[0], out_misc.at[1])
    top_out.start()
    tops_copy.wait_send()
    all_of(ur_v, 4).wait_send()
    all_of(fother_v, 5).wait_send()
    all_of(er_v.at[1], 7).wait_send()
    mid_out.wait()
    top_out.wait()
    all_of(fin_v, 6).wait()
    apex_out = pltpu.make_async_copy(fin_v, apex_o, out_misc.at[2])
    apex_out.start()
    apex_out.wait()


def place(leaf_i, mid_i, top_i, apex_i, leaf_o, mid_o, top_o, apex_o, sems):
    pairs = [(leaf_i.at[l], leaf_o.at[l]) for l in range(N_LEAF)]
    pairs += [(mid_i, mid_o), (top_i, top_o), (apex_i, apex_o)]
    copies = [pltpu.make_async_copy(s, d, sems.at[i]) for i, (s, d) in enumerate(pairs)]
    for copy in copies:
        copy.start()
    for copy in copies:
        copy.wait()


def per_device(*args):
    (
        leaf_rhs, leaf_inv, leaf_lower_mid, leaf_lower_coupling, leaf_parent, leaf_pattern,
        mid_rhs, parent_diagonal_inverse, mid_lower, mid_pattern, top_rhs, top_inv, top_lower,
        apex_rhs, apex_inv, apex_lower,
    ) = args
    smem = pl.BlockSpec(memory_space=pltpu.SMEM)
    anywhere = pl.BlockSpec(memory_space=pl.ANY)
    hbm = pl.BlockSpec(memory_space=pltpu.HBM)
    V = pltpu.VMEM
    D = pltpu.SemaphoreType.DMA
    scratch = [
        V((8, 256, 512), F32),
        V((8, 128, 512), BF16),
        V((512, 1024), BF16),
        V((3, 512, 1024), BF16),
        V((256, 128), F32),
        V((128, 512), BF16),
        V((3, 512, 128), BF16),
        V((16, 512), F32),
        V((128, 512), BF16),
        V((2, 512, 128), BF16),
        V((2, 16, 512), F32),
        V((2, 128, 512), BF16),
        V((512, 128), BF16),
        V((8, 256, 128), F32),
        V((256, 1024), BF16),
        V((3, 16, 1024), BF16),
        V((16, 1024), F32),
        V((3, 256, 512), F32),
        V((8, ROWS_Y, 128), BF16),
        V((8, 2, ROWS_Y // 2, 128), BF16),
        V((8, 2, ROWS_Y, 128), BF16),
        V((8, 2, ROWS_Y, 128), BF16),
        V((8, ROWS_Y, 128), BF16),
        V((8, ROWS_Y, 128), BF16),
        V((8, 8, 128), F32),
        V((8, 8, 128), F32),
        V((8, ROWS_Y, 128), F32),
        V((8, ROWS_Y, 128), BF16),
        V((7, ROWS_Y, 128), BF16),
        V((8, ROWS_Z, 512), BF16),
        V((8, ROWS_Z, 512), BF16),
        V((8, ROWS_Z, 512), F32),
        V((2, 4, 2, ROWS_Z // 2, 512), BF16),
        V((2, 4, 2, ROWS_Z // 2, 512), BF16),
        V((4, ROWS_Z, 128), BF16),
        V((3, ROWS_Z, 128), BF16),
        V((4, 256, 128), BF16),
        V((256, 128), F32),
        V((3, 128, 512), BF16),
        V((3, 128, 512), BF16),
        V((3, 128, 512), F32),
        V((3, 128, 512), BF16),
        V((3, 7, 16, 512), BF16),
        V((16, 512), BF16),
        V((3, 16, 512), BF16),
        V((256, 128), F32),
        V((16, 512), BF16),
        V((7, 16, 512), BF16),
        V((2, 16, 512), BF16),
        V((2, 3, 16, 512), BF16),
        V((16, 512), BF16),
        V((7, 16, 512), BF16),
        V((16, 128), F32),
        V((16, 128), F32),
        V((3, 16, 128), F32),
        V((3, 64, 128), F32),
        D((8, 4)),
        D((11,)),
        D((8,)),
        D((3,)),
        D((8, 2)),
        D((8, 2)),
        D((8, 2)),
        D((8, 2)),
        D((8,)),
        D((8,)),
        D((2,)),
        D((8,)),
        D((8,)),
        D((2,)),
        D((2, 4, 2)),
        D((2, 4, 2)),
        D((3,)),
        D((3,)),
        D((2, 3)),
        D((2, 3)),
        D((3,)),
        D((3,)),
        D((3,)),
        D((3,)),
        D((9,)),
        D((9,)),
    ]
    solved = pl.pallas_call(
        kernel,
        out_shape=(
            jax.ShapeDtypeStruct((8, 256, 128), F32),
            jax.ShapeDtypeStruct((1, 256, 128), F32),
            jax.ShapeDtypeStruct((1, 256, 128), F32),
            jax.ShapeDtypeStruct((3, 64, 128), F32),
        ),
        in_specs=[smem] * 3 + [hbm] * 13,
        out_specs=(anywhere,) * 4,
        scratch_shapes=scratch,
        compiler_params=pltpu.CompilerParams(
            collective_id=0, has_side_effects=True, vmem_limit_bytes=56 * 1024 * 1024
        ),
        name="tree_solve",
    )(
        leaf_parent, leaf_pattern.T, mid_pattern, leaf_rhs, leaf_inv, leaf_lower_mid,
        leaf_lower_coupling, mid_rhs, parent_diagonal_inverse, mid_lower, top_rhs, top_inv,
        top_lower, apex_rhs, apex_inv, apex_lower,
    )
    return pl.pallas_call(
        place,
        out_shape=[jax.ShapeDtypeStruct(x.shape, x.dtype) for x in solved],
        in_specs=[pl.BlockSpec(memory_space=V)] * 4,
        out_specs=[anywhere] * 4,
        scratch_shapes=[D((11,))],
        compiler_params=pltpu.CompilerParams(vmem_limit_bytes=56 * 1024 * 1024),
        name="place",
    )(*solved)


def solution(mesh):
    placed = (
        P(("gz", "col"), None, None),
        P(("gz", "col"), "row", None),
        P(("gz", "col"), None, "row"),
        P(("gz", "col"), None, None, "row"),
        P(("gz", "col")),
        P(("gz", "col"), None),
        P(("gz", "col"), None, None),
        P(("gz", "col"), "row", None),
        P(("gz", "col"), None, None, "row"),
        P(("gz", "col"), None),
        P("gz", None, None),
        P("gz", "row", None),
        P("gz", None, None, "row"),
        P(),
        P(None, "row", None),
        P(None, None, "row"),
    )
    return jax.shard_map(
        per_device,
        mesh=mesh,
        in_specs=placed,
        out_specs=(
            P(("gz", "col"), None, "row"),
            P(("gz", "col"), None, "row"),
            P("gz", None, "row"),
            P(None, "gz", "row"),
        ),
        check_vma=False,
    )
```

```python
import jax
import jax.numpy as jnp
from jax import lax
from jax.experimental import pallas as pl
from jax.experimental.pallas import tpu as pltpu
from jax.sharding import PartitionSpec as P

MESH = pl.DeviceIdType.MESH
F32 = jnp.float32
BF16 = jnp.bfloat16
N_LEAF = 8
SLICE = 128
HALF = 128
ROWS_Y = 64
ROWS_Z = 256 - ROWS_Y
PIECES = (48, 48, 48, 48)
SHARE = 16


def dot_nt(a, b):
    return lax.dot_general(a, b, (((1,), (1,)), ((), ())), preferred_element_type=F32)


def send(src, dst, send_sem, recv_sem, where):
    return pltpu.make_async_remote_copy(
        src_ref=src,
        dst_ref=dst,
        send_sem=send_sem,
        recv_sem=recv_sem,
        device_id=where,
        device_id_type=MESH,
    )


def kernel(
    parent_s,
    pattern_s,
    midpat_s,
    rhs_h,
    inv_h,
    lm_h,
    lc_h,
    midrhs_h,
    pinv_h,
    midl_h,
    toprhs_h,
    topinv_h,
    topl_h,
    apexrhs_h,
    apexinv_h,
    apexl_h,
    leaf_o,
    mid_o,
    top_o,
    apex_o,
    rhs_v,
    inv_v,
    lm_v,
    lc_v,
    midrhs_v,
    pinv_v,
    midl_v,
    toprhs_v,
    topinv_v,
    topl_v,
    apexrhs_v,
    apexinv_v,
    apexl_v,
    sol_v,
    rnd_v,
    weight_v,
    pidrow_v,
    up_v,
    y_s,
    y_own,
    y_r,
    part_v,
    sib_v,
    pid_v,
    pidsib_v,
    acc_v,
    yz_s,
    yz_r,
    pairs_s,
    pairs_r,
    wide_v,
    zsum_s,
    zsum_r,
    rs_s,
    rs_r,
    last_s,
    last_r,
    mt_v,
    msol_v,
    csend_v,
    crecv_v,
    ownp_v,
    zsc_v,
    zin_v,
    rsend_v,
    rrecv_v,
    tops_v,
    q1_v,
    q1r_v,
    e_v,
    er_v,
    u_v,
    ur_v,
    fsend_v,
    fother_v,
    fins_v,
    fin_v,
    ld_leaf,
    ld_misc,
    out_leaf,
    out_misc,
    y_ss,
    y_rs,
    sib_ss,
    sib_rs,
    pid_sem,
    pairs_ss,
    pairs_rs,
    yz_sem,
    zsum_ss,
    zsum_rs,
    rs_sem,
    last_ss,
    last_rs,
    mt_ss,
    mt_rs,
    c_ss,
    c_rs,
    zin_ss,
    zin_rs,
    x_ss,
    x_rs,
):
    g = lax.axis_index("gz")
    r = lax.axis_index("row")
    c = lax.axis_index("col")
    z, core = c // 2, c % 2
    pair = g // 2
    mate = g + 1 - 2 * (g % 2)
    facing = 3 - g
    block = core * 128 + z * SHARE
    sibling = {"col": 2 * z + (1 - core)}
    ahead = (r + 1) % 4

    def rows(start, count, unit):
        return pl.ds(pl.multiple_of(start, unit), count)

    def slab(index):
        return rows(index * SLICE, SLICE, SLICE)

    def leaf_loads(l):
        return (
            pltpu.make_async_copy(rhs_h.at[l], rhs_v.at[l], ld_leaf.at[l, 0]),
            pltpu.make_async_copy(inv_h.at[l], inv_v.at[l], ld_leaf.at[l, 1]),
        )

    def lower_load(l):
        return pltpu.make_async_copy(lm_h.at[l], lm_v.at[:, slab(l)], ld_leaf.at[l, 2])

    def coupling_load(l):
        return pltpu.make_async_copy(lc_h.at[l], lc_v.at[:, :, slab(l)], ld_leaf.at[l, 3])

    misc = (
        (midrhs_h.at[0, :, slab(r)], midrhs_v),
        (pinv_h.at[0], pinv_v),
        (midl_h.at[0], midl_v),
        (toprhs_h.at[0, rows(block, SHARE, SHARE), :], toprhs_v),
        (topinv_h.at[0], topinv_v),
        (topl_h.at[0], topl_v),
        (apexrhs_h.at[pair, rows(block, SHARE, SHARE), :], apexrhs_v.at[0]),
        (apexrhs_h.at[2, rows(block, SHARE, SHARE), :], apexrhs_v.at[1]),
        (apexinv_h.at[pair], apexinv_v.at[0]),
        (apexinv_h.at[2], apexinv_v.at[1]),
        (apexl_h.at[pair], apexl_v),
    )
    misc = [pltpu.make_async_copy(s, d, ld_misc.at[i]) for i, (s, d) in enumerate(misc)]

    @pl.loop(0, N_LEAF)
    def _(l):
        for copy in leaf_loads(l):
            copy.start()

    barrier = pltpu.get_barrier_semaphore()

    def greet(where):
        pl.semaphore_signal(barrier, inc=1, device_id=where, device_id_type=MESH)

    greet(sibling)
    for apart in range(1, 8):
        greet({"col": 2 * ((z + apart) % 8) + core})
    for apart in range(1, 4):
        greet({"row": (r + apart) % 4})
    for apart in range(4):
        greet({"gz": mate, "row": (r + apart) % 4})
        greet({"gz": facing, "row": (r + apart) % 4})
    greet({"gz": (g + 2) % 4})
    for apart in (1, 7):
        for turn in (1, 2, 3):
            greet({"row": (r + turn) % 4, "col": 2 * ((z + apart) % 8) + core})
    for i in range(4):
        giver = (g % 2) * 4 + i
        dz = (z - giver + 8) % 8
        passed = (dz + 6) // 7 + (dz + 4) // 7 + (dz + 1) // 7
        greet({"gz": (g + 6 - passed) % 4, "col": 2 * giver + g // 2})

    holder = core * 2 + z // 4
    turned = (g - holder + 4) % 4
    layers_off = turned - 2 * (turned // 3)

    @pl.loop(0, N_LEAF)
    def _(l):
        lower_load(l).start()

    @pl.loop(0, N_LEAF)
    def _(l):
        parent = parent_s[l].astype(F32)
        pid_v[l] = jnp.full((8, 128), parent, F32)
        pidrow_v[:, slab(l)] = jnp.full((16, 128), parent, F32)
        for k in range(3):
            weight_v[k, :, slab(l)] = jnp.full((16, 128), pattern_s[k, l].astype(F32), F32).astype(
                BF16
            )

    def leaf_out(l):
        return pltpu.make_async_copy(sol_v.at[l], leaf_o.at[l], out_leaf.at[l])

    @pl.loop(0, N_LEAF)
    def _(l):
        for copy in leaf_loads(l):
            copy.wait()
        solved = dot_nt(rhs_v[l].astype(BF16), inv_v[l])
        sol_v[l] = solved
        rnd_v[:, slab(l)] = solved.astype(BF16)
        leaf_out(l).start()

    pl.semaphore_wait(barrier, 26 + 6 - 2 * layers_off)

    pid_copy = send(pid_v, pidsib_v, pid_sem.at[0], pid_sem.at[1], sibling)
    pid_copy.start()

    def y_copy(l, apart):
        return send(
            y_s.at[l, (r + apart) % 4], y_r.at[l, apart - 1], y_ss.at[l], y_rs.at[l],
            {"row": (r + apart) % 4},
        )

    def y_all(l):
        return send(y_r.at[l], y_r.at[l], y_ss.at[l], y_rs.at[l], sibling)

    def sib_copy(l):
        return send(part_v.at[l], sib_v.at[l], sib_ss.at[l], sib_rs.at[l], sibling)

    @pl.loop(0, N_LEAF)
    def _(l):
        lower_load(l).wait()
        terms = dot_nt(rnd_v[:ROWS_Y, slab(l)], lm_v[:, slab(l)])
        for i in range(4):
            term = terms[:, i * SLICE : (i + 1) * SLICE]
            y_s[l, i] = term.astype(BF16)
            y_own[l, i] = term
        for apart in (2, 1, 3):
            y_copy(l, apart).start()

    @pl.loop(0, N_LEAF)
    def _(l):
        coupling_load(l).start()

    for copy in misc:
        copy.start()

    def pairs_copy(t):
        return send(pairs_s.at[t], pairs_r.at[t], pairs_ss.at[t], pairs_rs.at[t], sibling)

    def masked(parent):
        hit = jnp.maximum(1.0 - jnp.abs(pidrow_v[...] - parent.astype(F32)), 0.0).astype(BF16)
        terms = rnd_v[ROWS_Y:].reshape(ROWS_Z // 16, 16, 1024) * hit[None]
        return terms.reshape(ROWS_Z, 1024)

    def in_turn(i):
        return (z + 4 + ((i + 1) // 2) * (1 - 2 * (i % 2))) % 8

    def pairs(first, last):
        @pl.loop(first, last)
        def _(i):
            t = in_turn(i)
            terms = jnp.concatenate([masked(2 * t + 1 - core), masked(2 * t + core)], axis=0)
            sums = dot_nt(terms, lm_v[...])
            pairs_s[t] = sums[:ROWS_Z].astype(BF16)
            pairs_copy(t).start()
            wide_v[t] = sums[ROWS_Z:]

    pairs(0, 3)

    def z_copy(buffers, way, dist, h):
        out, into, send_sem, recv_sem = buffers
        at = (way, dist - 2, pl.ds(*pieces[h]))
        step = 1 if way == 0 else 7
        return send(
            out.at[at], into.at[at], send_sem.at[way, dist - 2, h],
            recv_sem.at[way, dist - 2, h],
            {"col": 2 * ((z + step) % 8) + core},
        )

    zsum = (zsum_s, zsum_r, zsum_ss, zsum_rs)
    pieces = []
    for size in PIECES:
        pieces.append((sum(p[1] for p in pieces), size))

    def flow(dist, late):
        return [
            (way, dist, h)
            for i in (0, 1)
            for way in (0, 1)
            for h in (2 * way + i if late else 2 - 2 * way + i,)
        ]

    def z_step(buffers, term_of, group):
        for way, dist, h in group:
            target = (z + dist) % 8 if way == 0 else (z + 8 - dist) % 8
            term = term_of(target, h)
            part = pl.ds(*pieces[h])
            if dist < 3 or (dist == 3 and h // 2 == way):
                z_copy(buffers, way, dist + 1, h).wait_recv()
                term = term + buffers[1][way, dist - 1, part].astype(F32)
            buffers[0][way, dist - 2, part] = term.astype(BF16)
            z_copy(buffers, way, dist, h).start()

    def z_term(target, h):
        part = pl.ds(*pieces[h])
        return wide_v[target, part] + pairs_r[target, part].astype(F32)

    def ready(t):
        pairs_copy(t % 8).wait_recv()

    ready(z + 4)
    z_step(zsum, z_term, flow(4, True))
    ready(z + 3)
    ready(z + 5)
    z_step(zsum, z_term, flow(3, False))

    pairs(3, 8)
    z_step(zsum, z_term, flow(3, True))

    acc_v[...] = jnp.zeros_like(acc_v)

    def gather_parents(*groups):
        for t in range(8):
            wanted = (2 * t + core).astype(F32)
            total = acc_v[t].reshape(ROWS_Y // 8, 8, 128)
            for pids, terms in groups:
                hit = jnp.maximum(1.0 - jnp.abs(pids - wanted), 0.0)
                total = total + terms.reshape(ROWS_Y // 8, 8, 128) * hit[None]
            acc_v[t] = total.reshape(ROWS_Y, 128)

    def collect(first, last):
        @pl.loop(first, last)
        def _(l):
            y_all(l).wait_recv()
            total = y_own[l, r]
            for i in range(3):
                total = total + y_r[l, i].astype(F32)
            part_v[l] = total.astype(BF16)
            sib_copy(l).start()

            @pl.when(l == 0)
            def _():
                gather_parents((pid_v[l], total))

            @pl.when(l > 0)
            def _():
                sib_copy(l - 1).wait_recv()
                gather_parents(
                    (pid_v[l], total), (pidsib_v[l - 1], sib_v[l - 1].astype(F32))
                )

    pid_copy.wait_recv()
    collect(0, 4)
    ready(z + 2)
    ready(z + 6)
    z_step(zsum, z_term, flow(2, False))
    collect(4, N_LEAF)
    sib_copy(N_LEAF - 1).wait_recv()
    gather_parents((pidsib_v[N_LEAF - 1], sib_v[N_LEAF - 1].astype(F32)))

    def yz_copy(apart):
        target = (z + apart) % 8
        return send(
            yz_s.at[target], yz_r.at[apart - 1], yz_sem.at[0], yz_sem.at[1],
            {"col": 2 * target + core},
        )

    yz_all = send(yz_r, yz_r, yz_sem.at[0], yz_sem.at[1], sibling)
    for apart in (4, 3, 5, 2, 6, 1, 7):
        target = (z + apart) % 8
        yz_s[target] = acc_v[target].astype(BF16)
        yz_copy(apart).start()
    z_step(zsum, z_term, flow(2, True))

    def own_copy(apart):
        return send(
            rs_s.at[(r + apart) % 4], rs_r.at[apart - 1], rs_sem.at[0], rs_sem.at[1],
            {"row": (r + apart) % 4},
        )

    rs_all = send(rs_r, rs_r, rs_sem.at[0], rs_sem.at[1], sibling)

    def last_copy(way, h, apart):
        target = (z + (1 if way == 0 else 7)) % 8
        return send(
            last_s.at[way, (r + apart) % 4, pl.ds(*pieces[h])],
            last_r.at[way, apart, pl.ds(*pieces[h])], last_ss.at[way, h], last_rs.at[way, h],
            {"row": (r + apart) % 4, "col": 2 * target + core},
        )

    def last_all(way, h):
        buffer = last_r.at[way, :, pl.ds(*pieces[h])]
        return send(buffer, buffer, last_ss.at[way, h], last_rs.at[way, h], sibling)

    def last_hop(group):
        for way, dist, h in group:
            term = z_term((z + 1) % 8 if way == 0 else (z + 7) % 8, h)
            z_copy(zsum, way, 2, h).wait_recv()
            part = pl.ds(*pieces[h])
            term = term + zsum_r[way, 0, part].astype(F32)
            for i in range(4):
                last_s[way, i, part] = term[:, i * SLICE : (i + 1) * SLICE].astype(BF16)
            for apart in (2, 1, 3, 0):
                last_copy(way, h, apart).start()

    ready(z)
    for h in range(4):
        total = z_term(z, h)
        wide_v[z, pl.ds(*pieces[h])] = total
        for i in range(4):
            rs_s[i, pl.ds(*pieces[h])] = total[:, i * SLICE : (i + 1) * SLICE].astype(BF16)
    for apart in (2, 1, 3):
        own_copy(apart).start()
    ready(z + 1)
    ready(z + 7)
    last_hop(flow(1, False))
    last_hop(flow(1, True))

    @pl.loop(0, N_LEAF)
    def _(l):
        coupling_load(l).wait()

    for k in range(3):
        terms = rnd_v[...].reshape(16, 16, 1024) * weight_v[k][None]
        up_v[k] = dot_nt(terms.reshape(256, 1024), lc_v[k])

    parts = ((0, ROWS_Y), (ROWS_Y, ROWS_Z))

    def mt_copy(p, apart):
        mine = mt_v.at[r, pl.ds(*parts[p])]
        return send(
            mine, mine, mt_ss.at[p, apart - 1], mt_rs.at[p, apart - 1], {"row": (r + apart) % 4}
        )

    def mt_arrival(p, apart):
        source = (r + 4 - apart) % 4
        theirs = mt_v.at[source, pl.ds(*parts[p])]
        return send(
            theirs, theirs, mt_ss.at[p, apart - 1], mt_rs.at[p, apart - 1], {"row": source}
        )

    misc[0].wait()
    yz_all.wait_recv()
    total = midrhs_v[:ROWS_Y] - acc_v[z]
    for i in range(7):
        total = total - yz_r[i].astype(F32)
    mt_v[r, :ROWS_Y] = total.astype(BF16)
    for apart in (2, 1, 3):
        mt_copy(0, apart).start()
    rs_all.wait_recv()
    total = midrhs_v[ROWS_Y:] - wide_v[z, :, slab(r)]
    for i in range(3):
        total = total - rs_r[i].astype(F32)
    for h, (start, size) in enumerate(pieces):
        part = total[start : start + size]
        for way in (0, 1):
            last_all(way, h).wait_recv()
            for i in range(4):
                part = part - last_r[way, i, start : start + size].astype(F32)
        mt_v[r, ROWS_Y + start : ROWS_Y + start + size] = part.astype(BF16)
    for apart in (2, 1, 3):
        mt_copy(1, apart).start()

    mid_weight = (None, midpat_s[0, 0].astype(F32), midpat_s[0, 1].astype(F32))

    def c_copy(k):
        return send(csend_v.at[k], crecv_v.at[k], c_ss.at[k], c_rs.at[k], sibling)

    misc[1].wait()
    misc[2].wait()
    for h in (0, 1):
        for apart in (1, 2, 3):
            if ROWS_Y < HALF and h == 0:
                mt_arrival(1, apart).wait_recv()
            if ROWS_Y >= HALF or h == 0:
                mt_arrival(h, apart).wait_recv()
        here = slice(h * HALF, (h + 1) * HALF)
        right = jnp.concatenate([mt_v[i, here] for i in range(4)], axis=1)
        solved = dot_nt(right, pinv_v[...])
        msol_v[here] = solved
        rounded = solved.astype(BF16)
        for k in range(3):
            term = dot_nt(rounded, midl_v[k])
            if k:
                term = term * mid_weight[k]
            up_v[k, here] = up_v[k, here] + term
            if h:
                csend_v[k] = up_v[k, rows((1 - core) * HALF, HALF, HALF)].astype(BF16)
                c_copy(k).start()
    mid_out = pltpu.make_async_copy(msol_v, mid_o.at[0], out_misc.at[0])
    mid_out.start()

    def zin_copy(k, apart):
        target = (z + apart) % 8
        return send(
            zsc_v.at[k, rows(target * SHARE, SHARE, SHARE)], zin_v.at[k, apart - 1],
            zin_ss.at[k], zin_rs.at[k], {"col": 2 * target + core},
        )

    def all_of(buffer, sem):
        return send(buffer, buffer, x_ss.at[sem], x_rs.at[sem], {"row": ahead})

    def zin_all(k):
        return send(zin_v.at[k], zin_v.at[k], zin_ss.at[k], zin_rs.at[k], {"row": ahead})

    for k in range(3):
        c_copy(k).wait_recv()
        total = up_v[k, rows(core * HALF, HALF, HALF)] + crecv_v[k].astype(F32)
        ownp_v[k] = total
        zsc_v[k] = total.astype(BF16)
        for apart in (4, 3, 5, 2, 6, 1, 7):
            zin_copy(k, apart).start()

    def share_sum(k):
        zin_all(k).wait_recv()
        total = ownp_v[k, rows(z * SHARE, SHARE, SHARE)]
        for i in range(7):
            total = total + zin_v[k, i].astype(F32)
        return total

    def to_rows(src, dst, sem):
        for apart in (2, 1, 3):
            send(
                src, dst.at[apart - 1], x_ss.at[sem], x_rs.at[sem], {"row": (r + apart) % 4}
            ).start()

    pid_copy.wait_send()

    @pl.loop(0, N_LEAF)
    def _(l):
        for copy in (y_all(l), sib_copy(l), pairs_copy(l)):
            copy.wait_send()
        leaf_out(l).wait()

    own = share_sum(0)
    rsend_v[...] = own.astype(BF16)
    to_rows(rsend_v, rrecv_v, 0)
    for i in range(3, 11):
        misc[i].wait()
    for way, dist, h in flow(4, True) + [
        at for dist in (3, 2) for late in (False, True) for at in flow(dist, late)
    ]:
        z_copy(zsum, way, dist, h).wait_send()
    for h in range(4):
        for way in (0, 1):
            last_all(way, h).wait_send()
    yz_all.wait_send()
    rs_all.wait_send()
    all_of(rrecv_v, 0).wait_recv()
    for i in range(3):
        own = own + rrecv_v[i].astype(F32)
    solved = dot_nt((toprhs_v[...] - own).astype(BF16), topinv_v[...])
    rounded = solved.astype(BF16)
    q1 = share_sum(1) + dot_nt(rounded, topl_v[0])
    q1_v[...] = q1.astype(BF16)

    def to_group(src, dst, sem, other):
        for layer in (1, 0):
            for apart in (2, 1, 3, 0):
                if layer or apart:
                    send(
                        src, dst.at[4 * layer + apart - 1], x_ss.at[sem], x_rs.at[sem],
                        {"gz": other if layer else g, "row": (r + apart) % 4},
                    ).start()

    to_group(q1_v, q1r_v, 1, mate)
    tops_v[rows(block, SHARE, SHARE)] = solved
    e = share_sum(2) + dot_nt(rounded, topl_v[1])
    e_v[0] = e.astype(BF16)
    to_rows(e_v.at[0], er_v.at[0], 2)
    for apart in range(1, 8):
        mine = tops_v.at[rows(block, SHARE, SHARE)]
        send(
            mine, mine, x_ss.at[3], x_rs.at[3], {"col": 2 * ((z + apart) % 8) + core}
        ).start()

    all_of(q1r_v, 1).wait_recv()
    for i in range(7):
        q1 = q1 + q1r_v[i].astype(F32)
    front = dot_nt((apexrhs_v[0] - q1).astype(BF16), apexinv_v[0])
    u = dot_nt(front.astype(BF16), apexl_v[...])
    u_v[...] = u.astype(BF16)
    to_group(u_v, ur_v, 4, facing)
    fsend_v[...] = front
    fins_v[pair] = front
    send(fsend_v, fother_v, x_ss.at[5], x_rs.at[5], {"gz": facing}).start()

    all_of(er_v.at[0], 2).wait_recv()
    for i in range(3):
        e = e + er_v[0, i].astype(F32)
    e_v[1] = e.astype(BF16)
    for apart in (1, 2, 3):
        send(
            e_v.at[1], er_v.at[1, apart - 1], x_ss.at[7], x_rs.at[7], {"gz": (g + apart) % 4}
        ).start()
    tops_seven = tops_v.at[rows(core * HALF, 112, HALF)]
    tops_eight = tops_v.at[rows(core * HALF, HALF, HALF)]
    tops_other = tops_v.at[rows((1 - core) * HALF, HALF, HALF)]
    all_of(tops_seven, 3).wait()
    tops_copy = send(tops_eight, tops_eight, x_ss.at[8], x_rs.at[8], sibling)
    tops_copy.start()
    for k in range(3):
        c_copy(k).wait_send()
        zin_all(k).wait_send()
    for p in (0, 1):
        for apart in (1, 2, 3):
            mt_copy(p, apart).wait_send()
    all_of(rrecv_v, 0).wait_send()
    all_of(q1r_v, 1).wait_send()
    all_of(er_v.at[0], 2).wait_send()

    all_of(er_v.at[1], 7).wait_recv()
    for i in range(3):
        e = e + er_v[1, i].astype(F32)
    last = apexrhs_v[1] - e - u
    all_of(fother_v, 5).wait_recv()
    fins_v[1 - pair] = fother_v[...]
    all_of(ur_v, 4).wait_recv()
    for i in range(7):
        last = last - ur_v[i].astype(F32)
    fins_v[2] = dot_nt(last.astype(BF16), apexinv_v[1])

    def final_copy(apart, other):
        return send(
            fins_v, fin_v.at[:, rows((z % 4) * SHARE, SHARE, SHARE)], x_ss.at[6], x_rs.at[6],
            {"gz": holder, "col": 2 * ((z + apart) % 8) + (1 - core if other else core)},
        )

    final_reach = ((4, 3, 5), (2, 1), (0,), (6, 7))
    for turn, reach in enumerate(final_reach):

        @pl.when(turned == turn)
        def _():
            for apart in reach:
                for other in (0, 1):
                    final_copy(apart, other).start()

    send(tops_eight, tops_other, x_ss.at[8], x_rs.at[8], sibling).wait_recv()
    top_out = pltpu.make_async_copy(tops_v, top_o.at[0], out_misc.at[1])
    top_out.start()
    tops_copy.wait_send()
    all_of(ur_v, 4).wait_send()
    all_of(fother_v, 5).wait_send()
    all_of(er_v.at[1], 7).wait_send()
    mid_out.wait()
    top_out.wait()
    for turn, reach in enumerate(final_reach):

        @pl.when(turned == turn)
        def _():
            for apart in reach:
                for other in (0, 1):
                    final_copy(apart, other).wait_send()

    all_of(fin_v, 6).wait_recv()
    apex_out = pltpu.make_async_copy(fin_v, apex_o, out_misc.at[2])
    apex_out.start()
    apex_out.wait()


def place(leaf_i, mid_i, top_i, apex_i, leaf_o, mid_o, top_o, apex_o, sems):
    pairs = [(leaf_i.at[l], leaf_o.at[l]) for l in range(N_LEAF)]
    pairs += [(mid_i, mid_o), (top_i, top_o), (apex_i, apex_o)]
    copies = [pltpu.make_async_copy(s, d, sems.at[i]) for i, (s, d) in enumerate(pairs)]
    for copy in copies:
        copy.start()
    for copy in copies:
        copy.wait()


def per_device(*args):
    (
        leaf_rhs, leaf_inv, leaf_lower_mid, leaf_lower_coupling, leaf_parent, leaf_pattern,
        mid_rhs, parent_diagonal_inverse, mid_lower, mid_pattern, top_rhs, top_inv, top_lower,
        apex_rhs, apex_inv, apex_lower,
    ) = args
    smem = pl.BlockSpec(memory_space=pltpu.SMEM)
    anywhere = pl.BlockSpec(memory_space=pl.ANY)
    hbm = pl.BlockSpec(memory_space=pltpu.HBM)
    V = pltpu.VMEM
    D = pltpu.SemaphoreType.DMA
    scratch = [
        V((8, 256, 512), F32),
        V((8, 128, 512), BF16),
        V((512, 1024), BF16),
        V((3, 512, 1024), BF16),
        V((256, 128), F32),
        V((128, 512), BF16),
        V((3, 512, 128), BF16),
        V((16, 512), F32),
        V((128, 512), BF16),
        V((2, 512, 128), BF16),
        V((2, 16, 512), F32),
        V((2, 128, 512), BF16),
        V((512, 128), BF16),
        V((8, 256, 128), F32),
        V((256, 1024), BF16),
        V((3, 16, 1024), BF16),
        V((16, 1024), F32),
        V((3, 256, 512), F32),
        V((8, 4, ROWS_Y, 128), BF16),
        V((8, 4, ROWS_Y, 128), F32),
        V((8, 3, ROWS_Y, 128), BF16),
        V((8, ROWS_Y, 128), BF16),
        V((8, ROWS_Y, 128), BF16),
        V((8, 8, 128), F32),
        V((8, 8, 128), F32),
        V((8, ROWS_Y, 128), F32),
        V((8, ROWS_Y, 128), BF16),
        V((7, ROWS_Y, 128), BF16),
        V((8, ROWS_Z, 512), BF16),
        V((8, ROWS_Z, 512), BF16),
        V((8, ROWS_Z, 512), F32),
        V((2, 3, ROWS_Z, 512), BF16),
        V((2, 3, ROWS_Z, 512), BF16),
        V((4, ROWS_Z, 128), BF16),
        V((3, ROWS_Z, 128), BF16),
        V((2, 4, ROWS_Z, 128), BF16),
        V((2, 4, ROWS_Z, 128), BF16),
        V((4, 256, 128), BF16),
        V((256, 128), F32),
        V((3, 128, 512), BF16),
        V((3, 128, 512), BF16),
        V((3, 128, 512), F32),
        V((3, 128, 512), BF16),
        V((3, 7, 16, 512), BF16),
        V((16, 512), BF16),
        V((3, 16, 512), BF16),
        V((256, 128), F32),
        V((16, 512), BF16),
        V((7, 16, 512), BF16),
        V((2, 16, 512), BF16),
        V((2, 3, 16, 512), BF16),
        V((16, 512), BF16),
        V((7, 16, 512), BF16),
        V((16, 128), F32),
        V((16, 128), F32),
        V((3, 16, 128), F32),
        V((3, 64, 128), F32),
        D((8, 4)),
        D((11,)),
        D((8,)),
        D((3,)),
        D((8,)),
        D((8,)),
        D((8,)),
        D((8,)),
        D((2,)),
        D((8,)),
        D((8,)),
        D((2,)),
        D((2, 3, 4)),
        D((2, 3, 4)),
        D((2,)),
        D((2, 4)),
        D((2, 4)),
        D((2, 3)),
        D((2, 3)),
        D((3,)),
        D((3,)),
        D((3,)),
        D((3,)),
        D((9,)),
        D((9,)),
    ]
    solved = pl.pallas_call(
        kernel,
        out_shape=(
            jax.ShapeDtypeStruct((8, 256, 128), F32),
            jax.ShapeDtypeStruct((1, 256, 128), F32),
            jax.ShapeDtypeStruct((1, 256, 128), F32),
            jax.ShapeDtypeStruct((3, 64, 128), F32),
        ),
        in_specs=[smem] * 3 + [hbm] * 13,
        out_specs=(anywhere,) * 4,
        scratch_shapes=scratch,
        compiler_params=pltpu.CompilerParams(
            collective_id=0, has_side_effects=True, vmem_limit_bytes=56 * 1024 * 1024
        ),
        name="tree_solve",
    )(
        leaf_parent, leaf_pattern.T, mid_pattern, leaf_rhs, leaf_inv, leaf_lower_mid,
        leaf_lower_coupling, mid_rhs, parent_diagonal_inverse, mid_lower, top_rhs, top_inv,
        top_lower, apex_rhs, apex_inv, apex_lower,
    )
    return pl.pallas_call(
        place,
        out_shape=[jax.ShapeDtypeStruct(x.shape, x.dtype) for x in solved],
        in_specs=[pl.BlockSpec(memory_space=V)] * 4,
        out_specs=[anywhere] * 4,
        scratch_shapes=[D((11,))],
        compiler_params=pltpu.CompilerParams(vmem_limit_bytes=56 * 1024 * 1024),
        name="place",
    )(*solved)


def solution(mesh):
    placed = (
        P(("gz", "col"), None, None),
        P(("gz", "col"), "row", None),
        P(("gz", "col"), None, "row"),
        P(("gz", "col"), None, None, "row"),
        P(("gz", "col")),
        P(("gz", "col"), None),
        P(("gz", "col"), None, None),
        P(("gz", "col"), "row", None),
        P(("gz", "col"), None, None, "row"),
        P(("gz", "col"), None),
        P("gz", None, None),
        P("gz", "row", None),
        P("gz", None, None, "row"),
        P(),
        P(None, "row", None),
        P(None, None, "row"),
    )
    return jax.shard_map(
        per_device,
        mesh=mesh,
        in_specs=placed,
        out_specs=(
            P(("gz", "col"), None, "row"),
            P(("gz", "col"), None, "row"),
            P("gz", None, "row"),
            P(None, "gz", "row"),
        ),
        check_vma=False,
    )
```

```python
import jax
import jax.numpy as jnp
from jax import lax
from jax.experimental import pallas as pl
from jax.experimental.pallas import tpu as pltpu
from jax.sharding import PartitionSpec as P

MESH = pl.DeviceIdType.MESH
F32 = jnp.float32
BF16 = jnp.bfloat16
N_LEAF = 8
SLICE = 128
HALF = 128
ROWS_Y = 64
ROWS_Z = 256 - ROWS_Y
PIECES = (48, 48, 48, 48)
SHARE = 16


def dot_nt(a, b):
    return lax.dot_general(a, b, (((1,), (1,)), ((), ())), preferred_element_type=F32)


def send(src, dst, send_sem, recv_sem, where):
    return pltpu.make_async_remote_copy(
        src_ref=src,
        dst_ref=dst,
        send_sem=send_sem,
        recv_sem=recv_sem,
        device_id=where,
        device_id_type=MESH,
    )


def kernel(
    parent_s,
    pattern_s,
    midpat_s,
    rhs_h,
    inv_h,
    lm_h,
    lc_h,
    midrhs_h,
    pinv_h,
    midl_h,
    toprhs_h,
    topinv_h,
    topl_h,
    apexrhs_h,
    apexinv_h,
    apexl_h,
    leaf_o,
    mid_o,
    top_o,
    apex_o,
    rhs_v,
    inv_v,
    lm_v,
    lc_v,
    midrhs_v,
    pinv_v,
    midl_v,
    toprhs_v,
    topinv_v,
    topl_v,
    apexrhs_v,
    apexinv_v,
    apexl_v,
    sol_v,
    rnd_v,
    weight_v,
    pidrow_v,
    up_v,
    y_s,
    y_own,
    y_r,
    part_v,
    sib_v,
    pid_v,
    pidsib_v,
    acc_v,
    yz_s,
    yz_r,
    pairs_s,
    pairs_r,
    wide_v,
    zsum_s,
    zsum_r,
    rs_s,
    rs_r,
    last_s,
    last_r,
    mt_v,
    msol_v,
    csend_v,
    crecv_v,
    ownp_v,
    zsc_v,
    zin_v,
    rsend_v,
    rrecv_v,
    tops_v,
    q1_v,
    q1r_v,
    e_v,
    er_v,
    u_v,
    ur_v,
    fsend_v,
    fother_v,
    fins_v,
    fin_v,
    ld_leaf,
    ld_misc,
    out_leaf,
    out_misc,
    y_ss,
    y_rs,
    sib_ss,
    sib_rs,
    pid_sem,
    pairs_ss,
    pairs_rs,
    yz_sem,
    zsum_ss,
    zsum_rs,
    rs_sem,
    last_ss,
    last_rs,
    mt_ss,
    mt_rs,
    c_ss,
    c_rs,
    zin_ss,
    zin_rs,
    x_ss,
    x_rs,
):
    g = lax.axis_index("gz")
    r = lax.axis_index("row")
    c = lax.axis_index("col")
    z, core = c // 2, c % 2
    pair = g // 2
    mate = g + 1 - 2 * (g % 2)
    facing = 3 - g
    block = core * 128 + z * SHARE
    sibling = {"col": 2 * z + (1 - core)}
    ahead = (r + 1) % 4

    def rows(start, count, unit):
        return pl.ds(pl.multiple_of(start, unit), count)

    def slab(index):
        return rows(index * SLICE, SLICE, SLICE)

    def leaf_loads(l):
        return (
            pltpu.make_async_copy(rhs_h.at[l], rhs_v.at[l], ld_leaf.at[l, 0]),
            pltpu.make_async_copy(inv_h.at[l], inv_v.at[l], ld_leaf.at[l, 1]),
        )

    def lower_load(l):
        return pltpu.make_async_copy(lm_h.at[l], lm_v.at[:, slab(l)], ld_leaf.at[l, 2])

    def coupling_load(l):
        return pltpu.make_async_copy(lc_h.at[l], lc_v.at[:, :, slab(l)], ld_leaf.at[l, 3])

    misc = (
        (midrhs_h.at[0, :, slab(r)], midrhs_v),
        (pinv_h.at[0], pinv_v),
        (midl_h.at[0], midl_v),
        (toprhs_h.at[0, rows(block, SHARE, SHARE), :], toprhs_v),
        (topinv_h.at[0], topinv_v),
        (topl_h.at[0], topl_v),
        (apexrhs_h.at[pair, rows(block, SHARE, SHARE), :], apexrhs_v.at[0]),
        (apexrhs_h.at[2, rows(block, SHARE, SHARE), :], apexrhs_v.at[1]),
        (apexinv_h.at[pair], apexinv_v.at[0]),
        (apexinv_h.at[2], apexinv_v.at[1]),
        (apexl_h.at[pair], apexl_v),
    )
    misc = [pltpu.make_async_copy(s, d, ld_misc.at[i]) for i, (s, d) in enumerate(misc)]

    @pl.loop(0, N_LEAF)
    def _(l):
        for copy in leaf_loads(l):
            copy.start()

    barrier = pltpu.get_barrier_semaphore()

    def greet(where):
        pl.semaphore_signal(barrier, inc=1, device_id=where, device_id_type=MESH)

    greet(sibling)
    for apart in range(1, 8):
        greet({"col": 2 * ((z + apart) % 8) + core})
    for apart in range(1, 4):
        greet({"row": (r + apart) % 4})
    for apart in range(4):
        greet({"gz": mate, "row": (r + apart) % 4})
        greet({"gz": facing, "row": (r + apart) % 4})
    greet({"gz": (g + 2) % 4})
    for apart in (1, 7):
        for turn in (1, 2, 3):
            greet({"row": (r + turn) % 4, "col": 2 * ((z + apart) % 8) + core})
    for i in range(4):
        giver = (g % 2) * 4 + i
        dz = (z - giver + 8) % 8
        passed = (dz + 6) // 7 + (dz + 4) // 7 + (dz + 1) // 7
        greet({"gz": (g + 6 - passed) % 4, "col": 2 * giver + g // 2})

    holder = core * 2 + z // 4
    turned = (g - holder + 4) % 4
    layers_off = turned - 2 * (turned // 3)

    @pl.loop(0, N_LEAF)
    def _(l):
        lower_load(l).start()

    @pl.loop(0, N_LEAF)
    def _(l):
        parent = parent_s[l].astype(F32)
        pid_v[l] = jnp.full((8, 128), parent, F32)
        pidrow_v[:, slab(l)] = jnp.full((16, 128), parent, F32)
        for k in range(3):
            weight_v[k, :, slab(l)] = jnp.full((16, 128), pattern_s[k, l].astype(F32), F32).astype(
                BF16
            )

    def leaf_out(l):
        return pltpu.make_async_copy(sol_v.at[l], leaf_o.at[l], out_leaf.at[l])

    @pl.loop(0, N_LEAF)
    def _(l):
        for copy in leaf_loads(l):
            copy.wait()
        solved = dot_nt(rhs_v[l].astype(BF16), inv_v[l])
        sol_v[l] = solved
        rnd_v[:, slab(l)] = solved.astype(BF16)
        leaf_out(l).start()

    pl.semaphore_wait(barrier, 26 + 6 - 2 * layers_off)

    pid_copy = send(pid_v, pidsib_v, pid_sem.at[0], pid_sem.at[1], sibling)
    pid_copy.start()

    def y_copy(l, apart):
        return send(
            y_s.at[l, (r + apart) % 4], y_r.at[l, apart - 1], y_ss.at[l], y_rs.at[l],
            {"row": (r + apart) % 4},
        )

    def y_all(l):
        return send(y_r.at[l], y_r.at[l], y_ss.at[l], y_rs.at[l], sibling)

    def sib_copy(l):
        return send(part_v.at[l], sib_v.at[l], sib_ss.at[l], sib_rs.at[l], sibling)

    def products(first, last):
        @pl.loop(first, last)
        def _(l):
            terms = dot_nt(rnd_v[:ROWS_Y, slab(l)], lm_v[:, slab(l)])
            for i in range(4):
                term = terms[:, i * SLICE : (i + 1) * SLICE]
                y_s[l, i] = term.astype(BF16)
                y_own[l, i] = term
            for apart in (2, 1, 3):
                y_copy(l, apart).start()

    def pairs_copy(t):
        return send(pairs_s.at[t], pairs_r.at[t], pairs_ss.at[t], pairs_rs.at[t], sibling)

    def masked(parent):
        hit = jnp.maximum(1.0 - jnp.abs(pidrow_v[...] - parent.astype(F32)), 0.0).astype(BF16)
        terms = rnd_v[ROWS_Y:].reshape(ROWS_Z // 16, 16, 1024) * hit[None]
        return terms.reshape(ROWS_Z, 1024)

    def in_turn(i):
        return (z + 4 + ((i + 1) // 2) * (1 - 2 * (i % 2))) % 8

    def pairs(first, last):
        @pl.loop(first, last)
        def _(i):
            t = in_turn(i)
            terms = jnp.concatenate([masked(2 * t + 1 - core), masked(2 * t + core)], axis=0)
            sums = dot_nt(terms, lm_v[...])
            pairs_s[t] = sums[:ROWS_Z].astype(BF16)
            pairs_copy(t).start()
            wide_v[t] = sums[ROWS_Z:]

    def z_copy(buffers, way, dist, h):
        out, into, send_sem, recv_sem = buffers
        at = (way, dist - 2, pl.ds(*pieces[h]))
        step = 1 if way == 0 else 7
        return send(
            out.at[at], into.at[at], send_sem.at[way, dist - 2, h],
            recv_sem.at[way, dist - 2, h],
            {"col": 2 * ((z + step) % 8) + core},
        )

    zsum = (zsum_s, zsum_r, zsum_ss, zsum_rs)
    pieces = []
    for size in PIECES:
        pieces.append((sum(p[1] for p in pieces), size))

    def flow(dist, late):
        return [
            (way, dist, h)
            for i in (0, 1)
            for way in (0, 1)
            for h in (2 * way + i if late else 2 - 2 * way + i,)
        ]

    def z_step(buffers, term_of, group):
        for way, dist, h in group:
            target = (z + dist) % 8 if way == 0 else (z + 8 - dist) % 8
            term = term_of(target, h)
            part = pl.ds(*pieces[h])
            if dist < 3 or (dist == 3 and h // 2 == way):
                z_copy(buffers, way, dist + 1, h).wait_recv()
                term = term + buffers[1][way, dist - 1, part].astype(F32)
            buffers[0][way, dist - 2, part] = term.astype(BF16)
            z_copy(buffers, way, dist, h).start()

    def z_term(target, h):
        part = pl.ds(*pieces[h])
        return wide_v[target, part] + pairs_r[target, part].astype(F32)

    def ready(t):
        pairs_copy(t % 8).wait_recv()

    @pl.loop(0, N_LEAF)
    def _(l):
        lower_load(l).wait()

    pairs(0, 3)
    products(0, 2)
    ready(z + 4)
    z_step(zsum, z_term, flow(4, True))
    ready(z + 3)
    ready(z + 5)
    z_step(zsum, z_term, flow(3, False))

    products(2, N_LEAF)
    pairs(3, 8)
    z_step(zsum, z_term, flow(3, True))

    @pl.loop(0, N_LEAF)
    def _(l):
        coupling_load(l).start()

    for copy in misc:
        copy.start()


    acc_v[...] = jnp.zeros_like(acc_v)

    def gather_parents(*groups):
        for t in range(8):
            wanted = (2 * t + core).astype(F32)
            total = acc_v[t].reshape(ROWS_Y // 8, 8, 128)
            for pids, terms in groups:
                hit = jnp.maximum(1.0 - jnp.abs(pids - wanted), 0.0)
                total = total + terms.reshape(ROWS_Y // 8, 8, 128) * hit[None]
            acc_v[t] = total.reshape(ROWS_Y, 128)

    def collect(first, last):
        @pl.loop(first, last)
        def _(l):
            y_all(l).wait_recv()
            total = y_own[l, r]
            for i in range(3):
                total = total + y_r[l, i].astype(F32)
            part_v[l] = total.astype(BF16)
            sib_copy(l).start()

            @pl.when(l == 0)
            def _():
                gather_parents((pid_v[l], total))

            @pl.when(l > 0)
            def _():
                sib_copy(l - 1).wait_recv()
                gather_parents(
                    (pid_v[l], total), (pidsib_v[l - 1], sib_v[l - 1].astype(F32))
                )

    pid_copy.wait_recv()
    collect(0, 4)
    ready(z + 2)
    ready(z + 6)
    z_step(zsum, z_term, flow(2, False))
    collect(4, N_LEAF)
    sib_copy(N_LEAF - 1).wait_recv()
    gather_parents((pidsib_v[N_LEAF - 1], sib_v[N_LEAF - 1].astype(F32)))

    def yz_copy(apart):
        target = (z + apart) % 8
        return send(
            yz_s.at[target], yz_r.at[apart - 1], yz_sem.at[0], yz_sem.at[1],
            {"col": 2 * target + core},
        )

    yz_all = send(yz_r, yz_r, yz_sem.at[0], yz_sem.at[1], sibling)
    for apart in (4, 3, 5, 2, 6, 1, 7):
        target = (z + apart) % 8
        yz_s[target] = acc_v[target].astype(BF16)
        yz_copy(apart).start()
    z_step(zsum, z_term, flow(2, True))

    def own_copy(apart):
        return send(
            rs_s.at[(r + apart) % 4], rs_r.at[apart - 1], rs_sem.at[0], rs_sem.at[1],
            {"row": (r + apart) % 4},
        )

    rs_all = send(rs_r, rs_r, rs_sem.at[0], rs_sem.at[1], sibling)

    def last_copy(way, h, apart):
        target = (z + (1 if way == 0 else 7)) % 8
        return send(
            last_s.at[way, (r + apart) % 4, pl.ds(*pieces[h])],
            last_r.at[way, apart, pl.ds(*pieces[h])], last_ss.at[way, h], last_rs.at[way, h],
            {"row": (r + apart) % 4, "col": 2 * target + core},
        )

    def last_all(way, h):
        buffer = last_r.at[way, :, pl.ds(*pieces[h])]
        return send(buffer, buffer, last_ss.at[way, h], last_rs.at[way, h], sibling)

    def last_hop(group):
        for way, dist, h in group:
            term = z_term((z + 1) % 8 if way == 0 else (z + 7) % 8, h)
            z_copy(zsum, way, 2, h).wait_recv()
            part = pl.ds(*pieces[h])
            term = term + zsum_r[way, 0, part].astype(F32)
            for i in range(4):
                last_s[way, i, part] = term[:, i * SLICE : (i + 1) * SLICE].astype(BF16)
            for apart in (2, 1, 3, 0):
                last_copy(way, h, apart).start()

    ready(z)
    for h in range(4):
        total = z_term(z, h)
        wide_v[z, pl.ds(*pieces[h])] = total
        for i in range(4):
            rs_s[i, pl.ds(*pieces[h])] = total[:, i * SLICE : (i + 1) * SLICE].astype(BF16)
    for apart in (2, 1, 3):
        own_copy(apart).start()
    ready(z + 1)
    ready(z + 7)
    last_hop(flow(1, False))
    last_hop(flow(1, True))

    @pl.loop(0, N_LEAF)
    def _(l):
        coupling_load(l).wait()

    for k in range(3):
        terms = rnd_v[...].reshape(16, 16, 1024) * weight_v[k][None]
        up_v[k] = dot_nt(terms.reshape(256, 1024), lc_v[k])

    parts = ((0, ROWS_Y), (ROWS_Y, ROWS_Z))

    def mt_copy(p, apart):
        mine = mt_v.at[r, pl.ds(*parts[p])]
        return send(
            mine, mine, mt_ss.at[p, apart - 1], mt_rs.at[p, apart - 1], {"row": (r + apart) % 4}
        )

    def mt_arrival(p, apart):
        source = (r + 4 - apart) % 4
        theirs = mt_v.at[source, pl.ds(*parts[p])]
        return send(
            theirs, theirs, mt_ss.at[p, apart - 1], mt_rs.at[p, apart - 1], {"row": source}
        )

    misc[0].wait()
    yz_all.wait_recv()
    total = midrhs_v[:ROWS_Y] - acc_v[z]
    for i in range(7):
        total = total - yz_r[i].astype(F32)
    mt_v[r, :ROWS_Y] = total.astype(BF16)
    for apart in (2, 1, 3):
        mt_copy(0, apart).start()
    rs_all.wait_recv()
    total = midrhs_v[ROWS_Y:] - wide_v[z, :, slab(r)]
    for i in range(3):
        total = total - rs_r[i].astype(F32)
    for h, (start, size) in enumerate(pieces):
        part = total[start : start + size]
        for way in (0, 1):
            last_all(way, h).wait_recv()
            for i in range(4):
                part = part - last_r[way, i, start : start + size].astype(F32)
        mt_v[r, ROWS_Y + start : ROWS_Y + start + size] = part.astype(BF16)
    for apart in (2, 1, 3):
        mt_copy(1, apart).start()

    mid_weight = (None, midpat_s[0, 0].astype(F32), midpat_s[0, 1].astype(F32))

    def c_copy(k):
        return send(csend_v.at[k], crecv_v.at[k], c_ss.at[k], c_rs.at[k], sibling)

    misc[1].wait()
    misc[2].wait()
    for h in (0, 1):
        for apart in (1, 2, 3):
            if ROWS_Y < HALF and h == 0:
                mt_arrival(1, apart).wait_recv()
            if ROWS_Y >= HALF or h == 0:
                mt_arrival(h, apart).wait_recv()
        here = slice(h * HALF, (h + 1) * HALF)
        right = jnp.concatenate([mt_v[i, here] for i in range(4)], axis=1)
        solved = dot_nt(right, pinv_v[...])
        msol_v[here] = solved
        rounded = solved.astype(BF16)
        for k in range(3):
            term = dot_nt(rounded, midl_v[k])
            if k:
                term = term * mid_weight[k]
            up_v[k, here] = up_v[k, here] + term
            if h:
                csend_v[k] = up_v[k, rows((1 - core) * HALF, HALF, HALF)].astype(BF16)
                c_copy(k).start()
    mid_out = pltpu.make_async_copy(msol_v, mid_o.at[0], out_misc.at[0])
    mid_out.start()

    def zin_copy(k, apart):
        target = (z + apart) % 8
        return send(
            zsc_v.at[k, rows(target * SHARE, SHARE, SHARE)], zin_v.at[k, apart - 1],
            zin_ss.at[k], zin_rs.at[k], {"col": 2 * target + core},
        )

    def all_of(buffer, sem):
        return send(buffer, buffer, x_ss.at[sem], x_rs.at[sem], {"row": ahead})

    def zin_all(k):
        return send(zin_v.at[k], zin_v.at[k], zin_ss.at[k], zin_rs.at[k], {"row": ahead})

    for k in range(3):
        c_copy(k).wait_recv()
        total = up_v[k, rows(core * HALF, HALF, HALF)] + crecv_v[k].astype(F32)
        ownp_v[k] = total
        zsc_v[k] = total.astype(BF16)
        for apart in (4, 3, 5, 2, 6, 1, 7):
            zin_copy(k, apart).start()

    def share_sum(k):
        zin_all(k).wait_recv()
        total = ownp_v[k, rows(z * SHARE, SHARE, SHARE)]
        for i in range(7):
            total = total + zin_v[k, i].astype(F32)
        return total

    def to_rows(src, dst, sem):
        for apart in (2, 1, 3):
            send(
                src, dst.at[apart - 1], x_ss.at[sem], x_rs.at[sem], {"row": (r + apart) % 4}
            ).start()

    pid_copy.wait_send()

    @pl.loop(0, N_LEAF)
    def _(l):
        for copy in (y_all(l), sib_copy(l), pairs_copy(l)):
            copy.wait_send()
        leaf_out(l).wait()

    own = share_sum(0)
    rsend_v[...] = own.astype(BF16)
    to_rows(rsend_v, rrecv_v, 0)
    for i in range(3, 11):
        misc[i].wait()
    for way, dist, h in flow(4, True) + [
        at for dist in (3, 2) for late in (False, True) for at in flow(dist, late)
    ]:
        z_copy(zsum, way, dist, h).wait_send()
    for h in range(4):
        for way in (0, 1):
            last_all(way, h).wait_send()
    yz_all.wait_send()
    rs_all.wait_send()
    all_of(rrecv_v, 0).wait_recv()
    for i in range(3):
        own = own + rrecv_v[i].astype(F32)
    solved = dot_nt((toprhs_v[...] - own).astype(BF16), topinv_v[...])
    rounded = solved.astype(BF16)
    q1 = share_sum(1) + dot_nt(rounded, topl_v[0])
    q1_v[...] = q1.astype(BF16)

    def to_group(src, dst, sem, other):
        for layer in (1, 0):
            for apart in (2, 1, 3, 0):
                if layer or apart:
                    send(
                        src, dst.at[4 * layer + apart - 1], x_ss.at[sem], x_rs.at[sem],
                        {"gz": other if layer else g, "row": (r + apart) % 4},
                    ).start()

    to_group(q1_v, q1r_v, 1, mate)
    tops_v[rows(block, SHARE, SHARE)] = solved
    e = share_sum(2) + dot_nt(rounded, topl_v[1])
    e_v[0] = e.astype(BF16)
    to_rows(e_v.at[0], er_v.at[0], 2)
    for apart in range(1, 8):
        mine = tops_v.at[rows(block, SHARE, SHARE)]
        send(
            mine, mine, x_ss.at[3], x_rs.at[3], {"col": 2 * ((z + apart) % 8) + core}
        ).start()

    all_of(q1r_v, 1).wait_recv()
    for i in range(7):
        q1 = q1 + q1r_v[i].astype(F32)
    front = dot_nt((apexrhs_v[0] - q1).astype(BF16), apexinv_v[0])
    u = dot_nt(front.astype(BF16), apexl_v[...])
    u_v[...] = u.astype(BF16)
    to_group(u_v, ur_v, 4, facing)
    fsend_v[...] = front
    fins_v[pair] = front
    send(fsend_v, fother_v, x_ss.at[5], x_rs.at[5], {"gz": facing}).start()

    all_of(er_v.at[0], 2).wait_recv()
    for i in range(3):
        e = e + er_v[0, i].astype(F32)
    e_v[1] = e.astype(BF16)
    for apart in (1, 2, 3):
        send(
            e_v.at[1], er_v.at[1, apart - 1], x_ss.at[7], x_rs.at[7], {"gz": (g + apart) % 4}
        ).start()
    tops_seven = tops_v.at[rows(core * HALF, 112, HALF)]
    tops_eight = tops_v.at[rows(core * HALF, HALF, HALF)]
    tops_other = tops_v.at[rows((1 - core) * HALF, HALF, HALF)]
    all_of(tops_seven, 3).wait()
    tops_copy = send(tops_eight, tops_eight, x_ss.at[8], x_rs.at[8], sibling)
    tops_copy.start()
    for k in range(3):
        c_copy(k).wait_send()
        zin_all(k).wait_send()
    for p in (0, 1):
        for apart in (1, 2, 3):
            mt_copy(p, apart).wait_send()
    all_of(rrecv_v, 0).wait_send()
    all_of(q1r_v, 1).wait_send()
    all_of(er_v.at[0], 2).wait_send()

    all_of(er_v.at[1], 7).wait_recv()
    for i in range(3):
        e = e + er_v[1, i].astype(F32)
    last = apexrhs_v[1] - e - u
    all_of(fother_v, 5).wait_recv()
    fins_v[1 - pair] = fother_v[...]
    all_of(ur_v, 4).wait_recv()
    for i in range(7):
        last = last - ur_v[i].astype(F32)
    fins_v[2] = dot_nt(last.astype(BF16), apexinv_v[1])

    def final_copy(apart, other):
        return send(
            fins_v, fin_v.at[:, rows((z % 4) * SHARE, SHARE, SHARE)], x_ss.at[6], x_rs.at[6],
            {"gz": holder, "col": 2 * ((z + apart) % 8) + (1 - core if other else core)},
        )

    final_reach = ((4, 3, 5), (2, 1), (0,), (6, 7))
    for turn, reach in enumerate(final_reach):

        @pl.when(turned == turn)
        def _():
            for apart in reach:
                for other in (0, 1):
                    final_copy(apart, other).start()

    send(tops_eight, tops_other, x_ss.at[8], x_rs.at[8], sibling).wait_recv()
    top_out = pltpu.make_async_copy(tops_v, top_o.at[0], out_misc.at[1])
    top_out.start()
    tops_copy.wait_send()
    all_of(ur_v, 4).wait_send()
    all_of(fother_v, 5).wait_send()
    all_of(er_v.at[1], 7).wait_send()
    mid_out.wait()
    top_out.wait()
    for turn, reach in enumerate(final_reach):

        @pl.when(turned == turn)
        def _():
            for apart in reach:
                for other in (0, 1):
                    final_copy(apart, other).wait_send()

    all_of(fin_v, 6).wait_recv()
    apex_out = pltpu.make_async_copy(fin_v, apex_o, out_misc.at[2])
    apex_out.start()
    apex_out.wait()


def place(leaf_i, mid_i, top_i, apex_i, leaf_o, mid_o, top_o, apex_o, *scratch):
    leaf_v, mid_v, top_v, apex_v, sems = scratch
    parts = [(leaf_i.at[l], leaf_v.at[l], leaf_o.at[l]) for l in range(N_LEAF)]
    parts += [(mid_i, mid_v, mid_o), (top_i, top_v, top_o), (apex_i, apex_v, apex_o)]
    loads = [pltpu.make_async_copy(s, v, sems.at[0, i]) for i, (s, v, _) in enumerate(parts)]
    stores = [pltpu.make_async_copy(v, d, sems.at[1, i]) for i, (_, v, d) in enumerate(parts)]
    for load in loads:
        load.start()
    for load, store in zip(loads, stores):
        load.wait()
        store.start()
    for store in stores:
        store.wait()


def per_device(*args):
    (
        leaf_rhs, leaf_inv, leaf_lower_mid, leaf_lower_coupling, leaf_parent, leaf_pattern,
        mid_rhs, parent_diagonal_inverse, mid_lower, mid_pattern, top_rhs, top_inv, top_lower,
        apex_rhs, apex_inv, apex_lower,
    ) = args
    smem = pl.BlockSpec(memory_space=pltpu.SMEM)
    anywhere = pl.BlockSpec(memory_space=pl.ANY)
    hbm = pl.BlockSpec(memory_space=pltpu.HBM)
    V = pltpu.VMEM
    D = pltpu.SemaphoreType.DMA
    scratch = [
        V((8, 256, 512), F32),
        V((8, 128, 512), BF16),
        V((512, 1024), BF16),
        V((3, 512, 1024), BF16),
        V((256, 128), F32),
        V((128, 512), BF16),
        V((3, 512, 128), BF16),
        V((16, 512), F32),
        V((128, 512), BF16),
        V((2, 512, 128), BF16),
        V((2, 16, 512), F32),
        V((2, 128, 512), BF16),
        V((512, 128), BF16),
        V((8, 256, 128), F32),
        V((256, 1024), BF16),
        V((3, 16, 1024), BF16),
        V((16, 1024), F32),
        V((3, 256, 512), F32),
        V((8, 4, ROWS_Y, 128), BF16),
        V((8, 4, ROWS_Y, 128), F32),
        V((8, 3, ROWS_Y, 128), BF16),
        V((8, ROWS_Y, 128), BF16),
        V((8, ROWS_Y, 128), BF16),
        V((8, 8, 128), F32),
        V((8, 8, 128), F32),
        V((8, ROWS_Y, 128), F32),
        V((8, ROWS_Y, 128), BF16),
        V((7, ROWS_Y, 128), BF16),
        V((8, ROWS_Z, 512), BF16),
        V((8, ROWS_Z, 512), BF16),
        V((8, ROWS_Z, 512), F32),
        V((2, 3, ROWS_Z, 512), BF16),
        V((2, 3, ROWS_Z, 512), BF16),
        V((4, ROWS_Z, 128), BF16),
        V((3, ROWS_Z, 128), BF16),
        V((2, 4, ROWS_Z, 128), BF16),
        V((2, 4, ROWS_Z, 128), BF16),
        V((4, 256, 128), BF16),
        V((256, 128), F32),
        V((3, 128, 512), BF16),
        V((3, 128, 512), BF16),
        V((3, 128, 512), F32),
        V((3, 128, 512), BF16),
        V((3, 7, 16, 512), BF16),
        V((16, 512), BF16),
        V((3, 16, 512), BF16),
        V((256, 128), F32),
        V((16, 512), BF16),
        V((7, 16, 512), BF16),
        V((2, 16, 512), BF16),
        V((2, 3, 16, 512), BF16),
        V((16, 512), BF16),
        V((7, 16, 512), BF16),
        V((16, 128), F32),
        V((16, 128), F32),
        V((3, 16, 128), F32),
        V((3, 64, 128), F32),
        D((8, 4)),
        D((11,)),
        D((8,)),
        D((3,)),
        D((8,)),
        D((8,)),
        D((8,)),
        D((8,)),
        D((2,)),
        D((8,)),
        D((8,)),
        D((2,)),
        D((2, 3, 4)),
        D((2, 3, 4)),
        D((2,)),
        D((2, 4)),
        D((2, 4)),
        D((2, 3)),
        D((2, 3)),
        D((3,)),
        D((3,)),
        D((3,)),
        D((3,)),
        D((10,)),
        D((10,)),
    ]
    solved = pl.pallas_call(
        kernel,
        out_shape=(
            jax.ShapeDtypeStruct((8, 256, 128), F32),
            jax.ShapeDtypeStruct((1, 256, 128), F32),
            jax.ShapeDtypeStruct((1, 256, 128), F32),
            jax.ShapeDtypeStruct((3, 64, 128), F32),
        ),
        in_specs=[smem] * 3 + [hbm] * 13,
        out_specs=(anywhere,) * 4,
        scratch_shapes=scratch,
        compiler_params=pltpu.CompilerParams(
            collective_id=0, has_side_effects=True, vmem_limit_bytes=56 * 1024 * 1024
        ),
        name="tree_solve",
    )(
        leaf_parent, leaf_pattern.T, mid_pattern, leaf_rhs, leaf_inv, leaf_lower_mid,
        leaf_lower_coupling, mid_rhs, parent_diagonal_inverse, mid_lower, top_rhs, top_inv,
        top_lower, apex_rhs, apex_inv, apex_lower,
    )
    return pl.pallas_call(
        place,
        out_shape=[jax.ShapeDtypeStruct(x.shape, x.dtype) for x in solved],
        in_specs=[anywhere] * 4,
        out_specs=[anywhere] * 4,
        scratch_shapes=[V(x.shape, x.dtype) for x in solved] + [D((2, 11))],
        compiler_params=pltpu.CompilerParams(vmem_limit_bytes=56 * 1024 * 1024),
        name="place",
    )(*solved)


def solution(mesh):
    placed = (
        P(("gz", "col"), None, None),
        P(("gz", "col"), "row", None),
        P(("gz", "col"), None, "row"),
        P(("gz", "col"), None, None, "row"),
        P(("gz", "col")),
        P(("gz", "col"), None),
        P(("gz", "col"), None, None),
        P(("gz", "col"), "row", None),
        P(("gz", "col"), None, None, "row"),
        P(("gz", "col"), None),
        P("gz", None, None),
        P("gz", "row", None),
        P("gz", None, None, "row"),
        P(),
        P(None, "row", None),
        P(None, None, "row"),
    )
    return jax.shard_map(
        per_device,
        mesh=mesh,
        in_specs=placed,
        out_specs=(
            P(("gz", "col"), None, "row"),
            P(("gz", "col"), None, "row"),
            P("gz", None, "row"),
            P(None, "gz", "row"),
        ),
        check_vma=False,
    )
```
